256 devices in a mesh: dp: 4 (over y), ctx: 64 (over z, x, core).
Axes of the slice: x: 4, y: 4, z: 8, core: 2. Of those that a mesh axis runs over, the one named last changes fastest.
Arguments:
- queries: bfloat16 [4, 8192, 768], P('dp', 'ctx'), may hold values from -6 to 6
- keys: bfloat16 [4, 8192, 768], P('dp', 'ctx'), may hold values from -6 to 6
- values: bfloat16 [4, 8192, 768], P('dp', 'ctx'), may hold values from -6 to 6
- out_grad: bfloat16 [4, 8192, 768], P('dp', 'ctx'), may hold values from -6 to 6
- picks: int32 [4, 128, 16], P('dp', 'ctx'), may hold values from 0 to 127, as said below
- conv_in: bfloat16 [4, 8192, 768], P('dp', 'ctx'), may hold values from -6 to 6
- conv_weight: float32 [31, 768], replicated, may hold values from -1 to 1
- conv_grad: bfloat16 [4, 8192, 768], P('dp', 'ctx'), may hold values from -16 to 16
Outputs:
- attention: bfloat16 [4, 8192, 768], P('dp', 'ctx')
- query_grad: bfloat16 [4, 8192, 768], P('dp', 'ctx')
- key_grad: bfloat16 [4, 8192, 768], P('dp', 'ctx')
- value_grad: bfloat16 [4, 8192, 768], P('dp', 'ctx')
- conv_out: bfloat16 [4, 8192, 768], P('dp', 'ctx')
- conv_in_grad: bfloat16 [4, 8192, 768], P('dp', 'ctx')
- weight_grad: float32 [31, 768], P(None, 'ctx')
The draws below stay inside these ranges and needn't reach their ends.
Inputs may be any that keep to these rules, and one draw needn't show every extreme that they name: picks[r, b, 0] = b; the other entries of a row are distinct and differ from b. Block c belongs to device c // 2 of ctx. The rows of one device's 2 query blocks name, from each other device, at most 1 distinct blocks, and some device names exactly 1 from some other device.
All inputs are finite; a program needn't handle non-finite values.
Results may differ from the reference program's by a relative error of at most 0.025.
Values may be sent and summed in bfloat16 or wider, within the bound.
No kernel may reach another device: no remote copies, remote signals or barrier semaphores. Data moves between devices by JAX's collectives and lax.ppermute only.
A program may use at most 192 MiB of HBM per device.

```python
import math
import jax
import jax.numpy as jnp
from jax import lax

D = 768
HEADS = 12
HEAD_DIM = 64
INNER = 768
KERNEL = 31
HALF = 15
BLOCK = 64
SEL = 16
QUERY_BLOCKS_PER = 2
CAP = 1
RECORDING_BLOCKS = 128
FRAMES = 8192
RECS = 4
N_CTX = 64


def draw_queries(key, part):
    query_key = jax.random.fold_in(key, 11)
    return jnp.clip(jax.random.normal(query_key, (RECS, FRAMES, INNER), jnp.float32), -6.0, 6.0).astype(jnp.bfloat16)


def draw_keys(key, part):
    key_stream = jax.random.fold_in(key, 13)
    return jnp.clip(jax.random.normal(key_stream, (RECS, FRAMES, INNER), jnp.float32), -6.0, 6.0).astype(jnp.bfloat16)


def draw_picks(key, part):
    key = jax.random.fold_in(key, 7)
    offer_key, hot_key, jitter_key = jax.random.split(key, 3)
    local_ids = jnp.arange(QUERY_BLOCKS_PER, dtype=jnp.int32)
    offer_score = jax.random.randint(offer_key, (RECS, N_CTX, N_CTX, QUERY_BLOCKS_PER), 0, 1 << 20) * QUERY_BLOCKS_PER + local_ids
    offer_rank = jnp.sum(offer_score[..., None, :] < offer_score[..., :, None], axis=-1)
    offered = (offer_rank < CAP).reshape(RECS, N_CTX, RECORDING_BLOCKS)
    offered_rows = jnp.repeat(offered, QUERY_BLOCKS_PER, axis=1)
    owner_score = jax.random.randint(hot_key, (RECS, N_CTX), 0, 1 << 20) * N_CTX + jnp.arange(N_CTX, dtype=jnp.int32)
    owner_position = jnp.sum(owner_score[:, None, :] > owner_score[:, :, None], axis=-1)
    popular_reward = jnp.where(owner_position < max(1, N_CTX // 8), 1024, 0).astype(jnp.int32)
    column_reward = jnp.repeat(popular_reward, QUERY_BLOCKS_PER, axis=1)[:, None, :]
    block_list = jnp.arange(RECORDING_BLOCKS, dtype=jnp.int32)
    same_device = block_list[:, None] // QUERY_BLOCKS_PER == block_list[None, :] // QUERY_BLOCKS_PER
    own_block = block_list[:, None] == block_list[None, :]
    candidate_block = offered_rows & ~same_device[None] | (same_device & ~own_block)[None]
    random_noise = jax.random.randint(jitter_key, (RECS, RECORDING_BLOCKS, RECORDING_BLOCKS), 0, 1024)
    score_values = jnp.where(candidate_block, (random_noise + column_reward) * RECORDING_BLOCKS + block_list, -1 - block_list)
    chosen = lax.top_k(score_values, SEL - 1)[1].astype(jnp.int32)
    own_column = jnp.broadcast_to(block_list[None, :, None], (RECS, RECORDING_BLOCKS, 1)).astype(jnp.int32)
    return jnp.concatenate([own_column, chosen], axis=-1)


def raised(values, rng, source, target, blocks, factor):
    owner, partner = [(jnp.arange(values.shape[dim]) // (values.shape[dim] // blocks)).reshape([-1 if axis == dim else 1 for axis in range(values.ndim)]) for dim in (source, target)]
    chosen = jax.random.permutation(rng, blocks)[partner]
    strong = (owner == chosen) | (owner == (partner + blocks // 2) % blocks)
    return jnp.where(strong, factor * values, values)


def level_of(stream_key, dims, shards, smallest, high):
    loudness, own = 1.0, jax.random.fold_in(stream_key, 6)
    for dim, shards_of in shards:
        steps = jnp.exp(jax.random.uniform(jax.random.fold_in(own, dim), (shards_of,), jnp.float32, smallest / len(shards), high / len(shards)))
        loudness = loudness * jnp.repeat(steps, dims[dim] // shards_of).reshape([-1 if axis == dim else 1 for axis in range(len(dims))])
    return loudness


def noise(own_key, dims, scale, bound, cuts=(), kind=jnp.bfloat16):
    factor_of = level_of(own_key, dims, cuts, -0.22, 0.18) if cuts else 1.0
    drawn = jax.random.normal(own_key, dims, jnp.float32) * scale * factor_of
    return jnp.minimum(jnp.maximum(drawn, -bound), bound).astype(kind)


def noise_with(own_key, shape, scale, most, shards, heavy, kind=jnp.bfloat16):
    entries = scale * jax.random.normal(own_key, shape, jnp.float32)
    if shards:
        entries = entries * level_of(own_key, shape, shards, -0.22, 0.18)
    return jnp.clip(raised(entries, jax.random.fold_in(own_key, 3), *heavy), -most, most).astype(kind)


def setup_inputs(seed: int = 0) -> dict:
    key_of = jax.random.split(jax.random.key(seed), 9)
    return {
        "queries": draw_queries(jax.random.fold_in(key_of[8], 71), 0),
        "keys": draw_keys(jax.random.fold_in(key_of[8], 71), 0),
        "values": noise(key_of[2], (RECS, FRAMES, INNER), 1.0, 6.0, ((0, 4), (1, 64))),
        "out_grad": noise(key_of[3], (RECS, FRAMES, INNER), 1.0, 6.0, ((0, 4), (1, 64))),
        "picks": draw_picks(jax.random.fold_in(key_of[8], 71), 0),
        "conv_in": noise(key_of[5], (RECS, FRAMES, D), 1.0, 6.0, ((0, 4), (1, 64))),
        "conv_weight": noise(key_of[6], (KERNEL, D), KERNEL ** -0.5, 1.0, (), jnp.float32),
        "conv_grad": noise_with(key_of[7], (RECS, FRAMES, D), 1.0, 16.0, ((0, 4), (1, 64)), (1, 2, 64, 4.0)),
    }


def attend_block(query_block, grad_block, gathered):
    row_count, inner = query_block.shape
    pick_count = gathered.shape[0]
    query_heads = query_block.astype(jnp.float32).reshape(row_count, HEADS, HEAD_DIM)
    grad_heads = grad_block.astype(jnp.float32).reshape(row_count, HEADS, HEAD_DIM)
    key_heads = gathered[:, :, :inner].astype(jnp.float32).reshape(-1, HEADS, HEAD_DIM)
    value_heads = gathered[:, :, inner:].astype(jnp.float32).reshape(-1, HEADS, HEAD_DIM)
    score_values = jnp.einsum('thd,khd->htk', query_heads, key_heads) / math.sqrt(HEAD_DIM)
    highest = lax.optimization_barrier(jnp.max(score_values, axis=2, keepdims=True))
    expanded = jnp.exp(score_values - highest)
    probabilities = expanded / lax.optimization_barrier(jnp.sum(expanded, axis=2, keepdims=True))
    weights = probabilities.astype(jnp.bfloat16)
    attended = jnp.einsum('htk,khd->thd', weights.astype(jnp.float32), value_heads)
    attended = attended.reshape(row_count, inner).astype(jnp.bfloat16)
    delta = lax.optimization_barrier(jnp.sum(grad_heads * attended.astype(jnp.float32).reshape(row_count, HEADS, HEAD_DIM), axis=2))
    value_part = jnp.einsum('htk,thd->khd', weights.astype(jnp.float32), grad_heads)
    prob_grad = jnp.einsum('thd,khd->htk', grad_heads, value_heads)
    score_grad = (probabilities * (prob_grad - delta.T[:, :, None])).astype(jnp.bfloat16)
    query_grad = jnp.einsum('htk,khd->thd', score_grad.astype(jnp.float32), key_heads) / math.sqrt(HEAD_DIM)
    query_grad = query_grad.reshape(row_count, inner).astype(jnp.bfloat16)
    key_part = jnp.einsum('htk,thd->khd', score_grad.astype(jnp.float32), query_heads) / math.sqrt(HEAD_DIM)
    parts = jnp.concatenate([key_part.reshape(pick_count, -1, inner), value_part.reshape(pick_count, -1, inner)], axis=2)
    return (attended, query_grad, parts)

def attend_recording(query_rows, grad_rows, key_rows, value_rows, pick_rows):
    key_values = jnp.concatenate([key_rows, value_rows], axis=1).reshape(RECORDING_BLOCKS, BLOCK, 2 * INNER)
    query_dev = query_rows.reshape(N_CTX, QUERY_BLOCKS_PER, BLOCK, INNER)
    grad_dev = grad_rows.reshape(N_CTX, QUERY_BLOCKS_PER, BLOCK, INNER)
    pick_dev = pick_rows.reshape(N_CTX, QUERY_BLOCKS_PER, SEL)

    def device_pass(accum, inputs):
        query_group, grad_group, pick_group = inputs

        def block_pass(items):
            return attend_block(items[0], items[1], key_values[items[2]])
        attended, query_grad, parts = lax.map(block_pass, (query_group, grad_group, pick_group))
        flat_ids = pick_group.reshape(-1).astype(jnp.int32)
        flat_parts = parts.reshape(QUERY_BLOCKS_PER * SEL, BLOCK, 2 * INNER)
        first_pos = jnp.argmax(flat_ids[:, None] == flat_ids[None, :], axis=1).astype(jnp.int32)
        merged = jnp.zeros_like(flat_parts).at[first_pos].add(flat_parts)
        rounded = lax.optimization_barrier(merged.astype(jnp.bfloat16)).astype(jnp.float32)
        return (accum.at[flat_ids].add(rounded), (attended, query_grad))
    start = jnp.zeros((RECORDING_BLOCKS, BLOCK, 2 * INNER), jnp.float32)
    accum, (attended, query_grad) = lax.scan(device_pass, start, (query_dev, grad_dev, pick_dev))
    key_grad = accum[:, :, :INNER].reshape(FRAMES, INNER).astype(jnp.bfloat16)
    value_grad = accum[:, :, INNER:].reshape(FRAMES, INNER).astype(jnp.bfloat16)
    return (attended.reshape(FRAMES, INNER), query_grad.reshape(FRAMES, INNER), key_grad, value_grad)

def convolve_recording(input_rows, weight, grad_rows):
    wide_input = jnp.pad(input_rows.astype(jnp.float32), ((HALF, HALF), (0, 0)))
    pre_activation = jnp.zeros((FRAMES, D), jnp.float32)
    for offset in range(KERNEL):
        pre_activation = pre_activation + weight[offset] * wide_input[offset:offset + FRAMES]
    gate = jax.nn.sigmoid(pre_activation)
    conv_out = (pre_activation * gate).astype(jnp.bfloat16)
    hidden_grad = (grad_rows.astype(jnp.float32) * gate * (1.0 + pre_activation * (1.0 - gate))).astype(jnp.bfloat16)
    grad_float = hidden_grad.astype(jnp.float32)
    wide_grad = jnp.pad(grad_float, ((HALF, HALF), (0, 0)))
    input_grad = jnp.zeros((FRAMES, D), jnp.float32)
    for offset in range(KERNEL):
        begin = KERNEL - 1 - offset
        input_grad = input_grad + weight[offset] * wide_grad[begin:begin + FRAMES]
    partial_grad = jnp.stack([lax.optimization_barrier(jnp.sum(wide_input[offset:offset + FRAMES] * grad_float, axis=0)) for offset in range(KERNEL)])
    return (conv_out, input_grad.astype(jnp.bfloat16), partial_grad)

def reference(queries, keys, values, out_grad, picks, conv_in, conv_weight, conv_grad):
    attention_list, query_list, key_list, value_list = ([], [], [], [])
    conv_list, input_list = ([], [])
    weight_total = jnp.zeros((KERNEL, D), jnp.float32)
    for record in range(RECS):
        attended, query_grad, key_grad, value_grad = attend_recording(queries[record], out_grad[record], keys[record], values[record], picks[record])
        attention_list.append(attended)
        query_list.append(query_grad)
        key_list.append(key_grad)
        value_list.append(value_grad)
        conv_out, input_grad, partial_grad = convolve_recording(conv_in[record], conv_weight, conv_grad[record])
        conv_list.append(conv_out)
        input_list.append(input_grad)
        weight_total = weight_total + partial_grad
    weight_grad = weight_total / math.sqrt(RECS * FRAMES)
    return (jnp.stack(attention_list), jnp.stack(query_list), jnp.stack(key_list), jnp.stack(value_list), jnp.stack(conv_list), jnp.stack(input_list), weight_grad)
```

```python
import functools
import math

import jax
import jax.numpy as jnp
from jax import lax
from jax.experimental import pallas as pl
from jax.experimental.pallas import tpu as pltpu
from jax.sharding import PartitionSpec as P

Z, X, CORES = 8, 4, 2
CHIPS = Z * X
BLOCK = 64
HEAD_DIM = 64
LANES = 128
SEL = 16
KERNEL = 31
ROWS = 4 * BLOCK
HALF_INNER = 384
PAIRS = HALF_INNER // LANES
EXTRA = 16
F32, BF16 = jnp.float32, jnp.bfloat16


def index_of(z, x, core):
    return (z * X + x) * CORES + core


PLACES = [(z, x, c) for z in range(Z) for x in range(X) for c in range(CORES)]


def along(axis, shift):
    if axis == "z":
        return [(index_of(z, x, c), index_of((z + shift) % Z, x, c)) for z, x, c in PLACES]
    return [(index_of(z, x, c), index_of(z, (x + shift) % X, c)) for z, x, c in PLACES]


def move(value, axis, shift):
    return lax.ppermute(value, "ctx", along(axis, shift))


def swap_cores(value):
    return lax.ppermute(value, "ctx", [(i, i ^ 1) for i in range(CHIPS * CORES)])


def plus(a, b):
    return (a.astype(F32) + b.astype(F32)).astype(BF16)


def gather_ring(block, axis, count, dim):
    half = block.shape[dim] // 2
    up = down = block
    ups, downs = [], []
    for _ in range(count // 2 - 1):
        up, down = move(up, axis, 1), move(down, axis, -1)
        ups.append(up)
        downs.append(down)
    far_up = move(lax.slice_in_dim(up, 0, half, axis=dim), axis, 1)
    far_down = move(lax.slice_in_dim(down, half, 2 * half, axis=dim), axis, -1)
    return [block] + downs + [(far_up, far_down)] + ups[::-1]


def scatter_ring(parts, axis, dim):
    count = len(parts)
    middle = count // 2
    length = parts[0].shape[dim]
    half = length // 2

    def low(v):
        return lax.slice_in_dim(v, 0, half, axis=dim)

    def high(v):
        return lax.slice_in_dim(v, half, length, axis=dim)

    up = move(low(parts[middle]), axis, 1)
    down = move(high(parts[middle]), axis, -1)
    above, below = parts[middle - 1], parts[middle + 1]
    up = jnp.concatenate([plus(low(above), up), high(above)], axis=dim)
    down = jnp.concatenate([low(below), plus(high(below), down)], axis=dim)
    for d in range(middle - 1, 0, -1):
        up, down = move(up, axis, 1), move(down, axis, -1)
        if d > 1:
            up, down = plus(up, parts[d - 1]), plus(down, parts[count - d + 1])
    return parts[0].astype(F32) + up.astype(F32) + down.astype(F32)


def attention_kernel(
    key_layout, value_layout, key_slots, value_slots, q_ref, g_ref, extra_ref, *refs
):
    key_count, value_count = len(key_layout), len(value_layout)
    key_pieces, refs = refs[:key_count], refs[key_count:]
    value_pieces, refs = refs[:value_count], refs[value_count:]
    o_ref, dq_ref, dk_ref, dv_ref, ktab, vtab, dk_acc, dv_acc, sems = refs
    pair = pl.program_id(0)

    def copies(p):
        jobs = []
        for which, (pieces, layout, table) in enumerate(
            ((key_pieces, key_layout, ktab), (value_pieces, value_layout, vtab))
        ):
            for piece, (start, size) in zip(pieces, layout):
                jobs.append(
                    pltpu.make_async_copy(
                        piece.at[:, :, pl.ds(p * LANES, LANES)],
                        table.at[p, pl.ds(start, size)],
                        sems.at[p, which],
                    )
                )
        return jobs

    @pl.when(pair == 0)
    def _():
        for p in range(PAIRS):
            for job in copies(p):
                job.start()

    dk_acc[...] = jnp.zeros_like(dk_acc)
    dv_acc[...] = jnp.zeros_like(dv_acc)

    for p in range(PAIRS):

        @pl.when(pair == p)
        def _(p=p):
            for job in copies(p):
                job.wait()

    left = lax.broadcasted_iota(jnp.int32, (BLOCK, LANES), 1) < HEAD_DIM

    def spread(v):
        zero = jnp.zeros_like(v)
        return jnp.concatenate([jnp.where(left, v, zero), jnp.where(left, zero, v)], axis=0)

    def merge(v):
        return jnp.where(left, v[:BLOCK], v[BLOCK:])

    nt = (((1,), (1,)), ((), ()))
    tn = (((0,), (0,)), ((), ()))

    def dot(a, b, dims):
        return lax.dot_general(a, b, dims, preferred_element_type=F32)

    scale = 1.0 / math.sqrt(HEAD_DIM)

    def visit(b, carry):
        rows = pl.ds(pl.multiple_of(b * BLOCK, BLOCK), BLOCK)
        kk = jnp.concatenate(
            [ktab[pair, key_slots[b, j] // 4, pl.ds(pl.multiple_of((key_slots[b, j] % 4) * BLOCK, BLOCK), BLOCK), :] for j in range(SEL)], axis=0
        )
        vv = jnp.concatenate(
            [vtab[pair, value_slots[b, j] // 4, pl.ds(pl.multiple_of((value_slots[b, j] % 4) * BLOCK, BLOCK), BLOCK), :] for j in range(SEL)], axis=0
        )
        query = spread((q_ref[rows, :].astype(F32) * scale).astype(BF16))
        grad = spread(g_ref[rows, :])
        scores = dot(kk, query, nt)
        scores = jnp.exp(scores - jnp.max(scores, axis=0, keepdims=True))
        probs = scores * (1.0 / jnp.sum(scores, axis=0, keepdims=True))
        weights = probs.astype(BF16)
        attended = merge(dot(weights, vv, tn)).astype(BF16)
        o_ref[rows, :] = attended
        product = grad.astype(F32) * jnp.concatenate([attended, attended], axis=0).astype(F32)
        delta = jnp.sum(product.T, axis=0, keepdims=True)
        slope = (probs * (dot(vv, grad, nt) - delta)).astype(BF16)
        dq_ref[rows, :] = (merge(dot(slope, kk, tn)) * scale).astype(BF16)
        key_part = dot(slope, query, (((1,), (0,)), ((), ())))
        value_part = dot(weights, grad, (((1,), (0,)), ((), ())))
        for j in range(SEL):
            part = slice(j * BLOCK, (j + 1) * BLOCK)
            k_at = pl.ds(pl.multiple_of(key_slots[b, j] * BLOCK, BLOCK), BLOCK)
            v_at = pl.ds(pl.multiple_of(value_slots[b, j] * BLOCK, BLOCK), BLOCK)
            dk_acc[k_at, :] = dk_acc[k_at, :] + key_part[part]
            dv_acc[v_at, :] = dv_acc[v_at, :] + value_part[part]
        return carry

    lax.fori_loop(0, 4, visit, 0)

    def emit(i, carry):
        at = pl.ds(pl.multiple_of(i * ROWS, ROWS), ROWS)
        dk_ref[i, pl.ds(0, ROWS), :] = dk_acc[at, :].astype(BF16)
        dv_ref[i] = dv_acc[at, :].astype(BF16)
        return carry

    lax.fori_loop(0, CHIPS, emit, 0)
    dk_ref[:, ROWS:, :] = extra_ref[...]


def attention(key_slots, value_slots, queries, grads, extra, key_pieces, value_pieces):
    def layout_of(pieces):
        out, start = [], 0
        for piece in pieces:
            out.append((start, piece.shape[0]))
            start += piece.shape[0]
        return out

    lane_block = lambda rows: pl.BlockSpec((rows, LANES), lambda p, *_: (0, p))
    chip_block = lambda rows: pl.BlockSpec((CHIPS, rows, LANES), lambda p, *_: (0, 0, p))
    count = len(key_pieces) + len(value_pieces)
    return pl.pallas_call(
        functools.partial(attention_kernel, layout_of(key_pieces), layout_of(value_pieces)),
        grid_spec=pltpu.PrefetchScalarGridSpec(
            num_scalar_prefetch=2,
            grid=(PAIRS,),
            in_specs=[lane_block(ROWS), lane_block(ROWS), chip_block(EXTRA)]
            + [pl.BlockSpec(memory_space=pl.ANY)] * count,
            out_specs=[
                lane_block(ROWS),
                lane_block(ROWS),
                chip_block(ROWS + EXTRA),
                chip_block(ROWS),
            ],
            scratch_shapes=[
                pltpu.VMEM((PAIRS, CHIPS, ROWS, LANES), BF16),
                pltpu.VMEM((PAIRS, CHIPS, ROWS, LANES), BF16),
                pltpu.VMEM((CHIPS * ROWS, LANES), F32),
                pltpu.VMEM((CHIPS * ROWS, LANES), F32),
                pltpu.SemaphoreType.DMA((PAIRS, 2)),
            ],
        ),
        out_shape=[
            jax.ShapeDtypeStruct((ROWS, HALF_INNER), BF16),
            jax.ShapeDtypeStruct((ROWS, HALF_INNER), BF16),
            jax.ShapeDtypeStruct((CHIPS, ROWS + EXTRA, HALF_INNER), BF16),
            jax.ShapeDtypeStruct((CHIPS, ROWS, HALF_INNER), BF16),
        ],
        compiler_params=pltpu.CompilerParams(
            dimension_semantics=("arbitrary",), vmem_limit_bytes=50 * 1024 * 1024
        ),
        cost_estimate=pl.CostEstimate(
            flops=2_400_000_000, bytes_accessed=26_000_000, transcendentals=1_600_000
        ),
        name="attend",
    )(key_slots, value_slots, queries, grads, extra, *key_pieces, *value_pieces)


def conv_kernel(x_ref, g_ref, before_ref, after_ref, w_ref, out_ref, dx_ref, dw_ref, xs, hs):
    frames = x_ref.shape[0]
    xs[0:32] = before_ref[0:32].astype(F32)
    xs[32 : 32 + frames] = x_ref[...].astype(F32)
    xs[32 + frames : 64 + frames] = after_ref[0:32].astype(F32)
    wide = frames + 32
    pre = jnp.zeros((wide, LANES), F32)
    for j in range(KERNEL):
        pre = pre + w_ref[j : j + 1, :] * xs[j + 1 : j + 1 + wide]
    gate = 1.0 / (1.0 + jnp.exp(-pre))
    out_ref[...] = (pre * gate)[16 : 16 + frames].astype(BF16)
    incoming = jnp.concatenate(
        [before_ref[32:48], g_ref[...], after_ref[32:48]], axis=0
    ).astype(F32)
    hidden = (incoming * gate * (1.0 + pre * (1.0 - gate))).astype(BF16).astype(F32)
    hs[...] = hidden
    total = jnp.zeros((frames, LANES), F32)
    for j in range(KERNEL):
        total = total + w_ref[j : j + 1, :] * hs[31 - j : 31 - j + frames]
    dx_ref[...] = total.astype(BF16)
    centre = hidden[16 : 16 + frames]
    for j in range(KERNEL):
        product = xs[j + 17 : j + 17 + frames] * centre
        dw_ref[j : j + 1, :] = jnp.sum(product, axis=0, keepdims=True)
    dw_ref[KERNEL:, :] = jnp.zeros((1, LANES), F32)


def convolve(x, g, before, after, weight):
    frames, channels = x.shape
    block = lambda rows: pl.BlockSpec((rows, LANES), lambda p: (0, p))
    return pl.pallas_call(
        conv_kernel,
        grid=(channels // LANES,),
        in_specs=[block(frames), block(frames), block(48), block(48), block(KERNEL)],
        out_specs=[block(frames), block(frames), block(KERNEL + 1)],
        out_shape=[
            jax.ShapeDtypeStruct((frames, channels), BF16),
            jax.ShapeDtypeStruct((frames, channels), BF16),
            jax.ShapeDtypeStruct((KERNEL + 1, channels), F32),
        ],
        scratch_shapes=[pltpu.VMEM((frames + 64, LANES), F32), pltpu.VMEM((frames + 32, LANES), F32)],
        compiler_params=pltpu.CompilerParams(dimension_semantics=("arbitrary",)),
        cost_estimate=pl.CostEstimate(
            flops=20_000_000, bytes_accessed=1_000_000, transcendentals=120_000
        ),
        name="conv",
    )(x, g, before, after, weight)


def body(queries, keys, values, out_grad, picks, conv_in, conv_weight, conv_grad):
    me = lax.axis_index("ctx")
    core = me % CORES
    my_x = (me // CORES) % X
    my_z = me // (CORES * X)
    frames = queries.shape[1]

    packed = jnp.stack([keys[0], values[0], queries[0], out_grad[0]])
    first, second = packed[:, :, :HALF_INNER], packed[:, :, HALF_INNER:]
    flip = core == 1
    kept = jnp.where(flip, second, first)
    given = jnp.where(flip, first, second)
    taken = swap_cores(given)
    chip = jnp.concatenate([kept, taken], axis=1)
    key_block, value_block, query_rows, grad_rows = chip[0], chip[1], chip[2], chip[3]

    key_row = jnp.stack(
        [key_block, move(key_block, "x", -1), move(key_block, "x", 2), move(key_block, "x", 1)]
    )
    value_near = gather_ring(value_block, "z", Z, 0)
    value_near[Z // 2] = jnp.concatenate(value_near[Z // 2], axis=0)
    value_column = jnp.stack(value_near)
    key_far = gather_ring(key_row, "z", Z, 0)
    value_far = gather_ring(value_column, "x", X, 0)
    key_pieces = key_far[: Z // 2] + list(key_far[Z // 2]) + key_far[Z // 2 + 1 :]
    value_pieces = value_far[: X // 2] + list(value_far[X // 2]) + value_far[X // 2 + 1 :]

    chosen = jnp.concatenate([picks[0], swap_cores(picks[0])], axis=0)
    owner = chosen // 2
    dz = (owner // (CORES * X) - my_z) % Z
    dx = ((owner // CORES) % X - my_x) % X
    inner = (owner % CORES != core) * 2 + chosen % 2
    key_slots = (dz * X + dx) * 4 + inner
    value_slots = (dx * Z + dz) * 4 + inner

    ends = CHIPS * CORES - 1
    tail = jnp.concatenate([conv_in[0, frames - 32 :], conv_grad[0, frames - 16 :]], axis=0)
    head = jnp.concatenate([conv_in[0, :32], conv_grad[0, :16]], axis=0)
    before = lax.ppermute(tail, "ctx", [(i, i + 1) for i in range(ends)])
    after = lax.ppermute(head, "ctx", [(i + 1, i) for i in range(ends)])
    conv_out, conv_dx, partial = convolve(conv_in[0], conv_grad[0], before, after, conv_weight)

    columns = conv_weight.shape[1] // (CHIPS * CORES)
    table = partial[:KERNEL].reshape(KERNEL, CHIPS, CORES, columns).transpose(2, 1, 0, 3)
    table = table.reshape(CORES, CHIPS, KERNEL * columns)
    share = jnp.where(flip, table[1], table[0]) + swap_cores(jnp.where(flip, table[0], table[1]))
    share = share + lax.ppermute(share, "dp", [(i, i ^ 1) for i in range(4)])
    share = share + lax.ppermute(share, "dp", [(i, i ^ 2) for i in range(4)])
    chips = jnp.arange(CHIPS, dtype=jnp.int32)
    order = ((chips // X + my_z) % Z) * X + (chips % X + my_x) % X
    share = share[order]
    extra = jnp.pad(
        share[:, None, :], ((0, 0), (0, EXTRA - 1), (0, HALF_INNER - KERNEL * columns))
    ).astype(BF16)

    attended, query_grad, key_parts, value_parts = attention(
        key_slots, value_slots, query_rows, grad_rows, extra, key_pieces, value_pieces
    )

    key_parts = key_parts.reshape(Z, X, ROWS + EXTRA, HALF_INNER)
    value_parts = value_parts.reshape(X, Z, ROWS, HALF_INNER)
    key_sum = scatter_ring([key_parts[d] for d in range(Z)], "z", 0)
    value_sum = scatter_ring([value_parts[d] for d in range(X)], "x", 0).astype(BF16)
    key_send = key_sum.astype(BF16)
    key_sum = (
        key_sum[0]
        + move(key_send[1], "x", 1).astype(F32)
        + move(key_send[2], "x", 2).astype(F32)
        + move(key_send[3], "x", -1).astype(F32)
    )
    value_sum = scatter_ring([value_sum[d] for d in range(Z)], "z", 0)
    key_total = key_sum[:ROWS].astype(BF16)
    value_total = value_sum.astype(BF16)
    weight_grad = key_sum[ROWS, : KERNEL * columns].reshape(KERNEL, columns) / math.sqrt(
        conv_in.shape[0] * lax.axis_size("dp") * frames * CHIPS * CORES
    )

    def whole(half):
        other = swap_cores(half[:, frames:])
        mine = half[:, :frames]
        return jnp.concatenate(
            [jnp.where(flip, other, mine), jnp.where(flip, mine, other)], axis=2
        )

    early = whole(jnp.stack([attended, query_grad]))
    late = whole(jnp.stack([key_total, value_total]))
    return (
        early[0][None],
        early[1][None],
        late[0][None],
        late[1][None],
        conv_out[None],
        conv_dx[None],
        weight_grad,
    )


def solution(mesh):
    rows = P("dp", "ctx", None)
    return jax.shard_map(
        body,
        mesh=mesh,
        in_specs=(rows, rows, rows, rows, rows, rows, P(), rows),
        out_specs=(rows, rows, rows, rows, rows, rows, P(None, "ctx")),
        check_vma=False,
    )
```

```python
import functools
import math

import jax
import jax.numpy as jnp
from jax import lax
from jax.experimental import pallas as pl
from jax.experimental.pallas import tpu as pltpu
from jax.sharding import PartitionSpec as P

Z, X, CORES = 8, 4, 2
CHIPS = Z * X
BLOCK = 64
HEAD_DIM = 64
LANES = 128
SEL = 16
KERNEL = 31
ROWS = 4 * BLOCK
HALF_INNER = 384
PAIRS = HALF_INNER // LANES
EXTRA = 16
TAIL = 16
TAPS = KERNEL + 1
CHANNELS = 768
WIDTH = CHANNELS // (Z * X * CORES)
SENT = ROWS + EXTRA + TAIL
F32, BF16 = jnp.float32, jnp.bfloat16


def index_of(z, x, core):
    return (z * X + x) * CORES + core


PLACES = [(z, x, c) for z in range(Z) for x in range(X) for c in range(CORES)]


def along(axis, shift):
    if axis == "z":
        return [(index_of(z, x, c), index_of((z + shift) % Z, x, c)) for z, x, c in PLACES]
    return [(index_of(z, x, c), index_of(z, (x + shift) % X, c)) for z, x, c in PLACES]


def move(value, axis, shift):
    return lax.ppermute(value, "ctx", along(axis, shift))


COLUMNS = [[index_of(z, x, c) for z in range(Z)] for x in range(X) for c in range(CORES)]


def after(value, *others):
    return lax.optimization_barrier((value, *others))[0]


def swap_cores(value):
    return lax.ppermute(value, "ctx", [(i, i ^ 1) for i in range(CHIPS * CORES)])


def plus(a, b):
    return (a.astype(F32) + b.astype(F32)).astype(BF16)


def scatter_ring(parts, axis, dim, last=()):
    count = len(parts)
    middle = count // 2
    length = parts[0].shape[dim]
    half = length // 2

    def low(v):
        return lax.slice_in_dim(v, 0, half, axis=dim)

    def high(v):
        return lax.slice_in_dim(v, half, length, axis=dim)

    up = move(low(parts[middle]), axis, 1)
    down = move(high(parts[middle]), axis, -1)
    above, below = parts[middle - 1], parts[middle + 1]
    up = jnp.concatenate([plus(low(above), up), high(above)], axis=dim)
    down = jnp.concatenate([low(below), plus(high(below), down)], axis=dim)
    for d in range(middle - 1, 0, -1):
        if d == 1 and last:
            up, down = after(up, *last), after(down, *last)
        up, down = move(up, axis, 1), move(down, axis, -1)
        if d > 1:
            up, down = plus(up, parts[d - 1]), plus(down, parts[count - d + 1])
    return parts[0].astype(F32) + up.astype(F32) + down.astype(F32)


def attention_kernel(
    slots, key_homes, value_homes, place, q_ref, g_ref, total_ref, table_ref,
    o_ref, dq_ref, dk_ref, dv_ref, pairs, taps, sems,
):
    pair = pl.program_id(0)

    def copies(p):
        lanes = pl.ds(pl.multiple_of(place[2] * HALF_INNER + p * LANES, LANES), LANES)
        return [
            pltpu.make_async_copy(
                table_ref.at[:, which, :, lanes],
                pairs.at[p, :, :, pl.ds(which * LANES, LANES)],
                sems.at[p, which],
            )
            for which in range(2)
        ]

    @pl.when(pair == 0)
    def _():
        for p in range(PAIRS):
            for job in copies(p):
                job.start()

    dk_ref[...] = jnp.zeros_like(dk_ref)
    dv_ref[...] = jnp.zeros_like(dv_ref)

    for p in range(PAIRS):

        @pl.when(pair == p)
        def _(p=p):
            for job in copies(p):
                job.wait()

    left = lax.broadcasted_iota(jnp.int32, (BLOCK, LANES), 1) < HEAD_DIM
    none = jnp.zeros((LANES, LANES), BF16)

    def spread(v):
        zero = jnp.zeros_like(v)
        return jnp.concatenate([jnp.where(left, v, zero), jnp.where(left, zero, v)], axis=0)

    def merge(v):
        return jnp.where(left, v[:BLOCK], v[BLOCK:])

    def dot(a, b, dims):
        return lax.dot_general(a, b, dims, preferred_element_type=F32)

    def add(ref, home, part):
        at = (home // 4, pl.ds(pl.multiple_of(home % 4 * BLOCK, BLOCK), BLOCK), slice(None))
        ref[at] = (ref[at].astype(F32) + part).astype(BF16)

    scale = 1.0 / math.sqrt(HEAD_DIM)

    def visit(b):
        rows = slice(b * BLOCK, (b + 1) * BLOCK)
        both = jnp.concatenate(
            [
                pairs[
                    pair,
                    slots[b, j] // 2,
                    pl.ds(pl.multiple_of(slots[b, j] % 2 * BLOCK, BLOCK), BLOCK),
                    :,
                ]
                for j in range(SEL)
            ],
            axis=0,
        )
        query = spread((q_ref[rows, :].astype(F32) * scale).astype(BF16))
        grad = spread(g_ref[rows, :])
        sides = jnp.concatenate(
            [jnp.concatenate([query, none], axis=1), jnp.concatenate([none, grad], axis=1)], axis=0
        )
        products = dot(both, sides, (((1,), (1,)), ((), ())))
        scores, prob_grad = products[:, :LANES], products[:, LANES:]
        scores = jnp.exp(scores - jnp.max(scores, axis=0, keepdims=True))
        probs = scores * (1.0 / jnp.sum(scores, axis=0, keepdims=True))
        delta = jnp.sum(probs * prob_grad, axis=0, keepdims=True)
        slope = probs * (prob_grad - delta)
        factors = jnp.concatenate([slope.astype(BF16), probs.astype(BF16)], axis=1)
        sums = dot(factors, both, (((0,), (0,)), ((), ())))
        dq_ref[rows, :] = (merge(sums[:LANES, :LANES]) * scale).astype(BF16)
        o_ref[rows, :] = merge(sums[LANES:, LANES:]).astype(BF16)
        parts = dot(factors, sides, (((1,), (0,)), ((), ())))
        for j in range(SEL):
            part = slice(j * BLOCK, (j + 1) * BLOCK)
            add(dk_ref, key_homes[b, j], parts[part, :LANES])
            add(dv_ref, value_homes[b, j], parts[part, LANES:])

    for b in range(4):
        visit(b)

    for i in range(CHIPS):
        dk_ref[i, ROWS + EXTRA :, :] = dv_ref[
            i % X * Z + lax.rem(i // X - place[0] + Z, Z), ROWS - TAIL :, :
        ]

    @pl.when(pair == 0)
    def _():
        for c in range(CHANNELS // LANES):
            part = slice(c * LANES, (c + 1) * LANES)
            taps[part] = total_ref[:, part].T
        odd = place[2] == 1
        blank = jnp.zeros((EXTRA, LANES - TAPS), F32)
        fill = jnp.zeros((EXTRA - WIDTH, TAPS), F32)

        def extra(i, carry):
            chip = (i // X) * X + lax.rem(i % X + place[1], X)
            both = taps[pl.ds(pl.multiple_of(chip * 2 * WIDTH, 2 * WIDTH), 2 * WIDTH)]
            mine = jnp.where(odd, both[WIDTH:], both[:WIDTH])
            mine = jnp.concatenate([jnp.concatenate([mine, fill], axis=0), blank], axis=1)
            dk_ref[i, pl.ds(ROWS, EXTRA), :] = mine.astype(BF16)
            return carry

        lax.fori_loop(0, CHIPS, extra, 0)


def attention(slots, place, queries, grads, total, table):
    owner = slots // 2
    z, x = owner // (CORES * X), owner // CORES % X
    dz, dx = (z - place[0]) % Z, (x - place[1]) % X
    inner = owner % CORES * 2 + slots % 2
    key_homes = (z * X + dx) * 4 + inner
    value_homes = (dx * Z + dz) * 4 + inner
    lane_block = lambda rows: pl.BlockSpec((rows, LANES), lambda p, *_: (0, p))
    chip_block = lambda rows: pl.BlockSpec((CHIPS, rows, LANES), lambda p, *_: (0, 0, p))
    return pl.pallas_call(
        attention_kernel,
        grid_spec=pltpu.PrefetchScalarGridSpec(
            num_scalar_prefetch=4,
            grid=(PAIRS,),
            in_specs=[
                lane_block(ROWS),
                lane_block(ROWS),
                pl.BlockSpec((TAPS, CHANNELS), lambda p, *_: (0, 0)),
                pl.BlockSpec(memory_space=pl.ANY),
            ],
            out_specs=[
                lane_block(ROWS),
                lane_block(ROWS),
                chip_block(SENT),
                chip_block(ROWS),
            ],
            scratch_shapes=[
                pltpu.VMEM((PAIRS, CHIPS * CORES, ROWS // CORES, 2 * LANES), BF16),
                pltpu.VMEM((CHANNELS, TAPS), F32),
                pltpu.SemaphoreType.DMA((PAIRS, 2)),
            ],
        ),
        out_shape=[
            jax.ShapeDtypeStruct((ROWS, HALF_INNER), BF16),
            jax.ShapeDtypeStruct((ROWS, HALF_INNER), BF16),
            jax.ShapeDtypeStruct((CHIPS, SENT, HALF_INNER), BF16),
            jax.ShapeDtypeStruct((CHIPS, ROWS, HALF_INNER), BF16),
        ],
        compiler_params=pltpu.CompilerParams(
            dimension_semantics=("arbitrary",), vmem_limit_bytes=50 * 1024 * 1024
        ),
        cost_estimate=pl.CostEstimate(
            flops=2_400_000_000, bytes_accessed=26_000_000, transcendentals=1_600_000
        ),
        name="attend",
    )(slots, key_homes, value_homes, place, queries, grads, total, table)


def conv_kernel(x_ref, g_ref, before_ref, after_ref, w_ref, out_ref, dx_ref, dw_ref, xs, hs):
    frames = x_ref.shape[0]
    xs[0:32] = before_ref[0:32].astype(F32)
    xs[32 : 32 + frames] = x_ref[...].astype(F32)
    xs[32 + frames : 64 + frames] = after_ref[0:32].astype(F32)
    wide = frames + 32
    pre = jnp.zeros((wide, LANES), F32)
    for j in range(KERNEL):
        pre = pre + w_ref[j : j + 1, :] * xs[j + 1 : j + 1 + wide]
    gate = 1.0 / (1.0 + jnp.exp(-pre))
    out_ref[...] = (pre * gate)[16 : 16 + frames].astype(BF16)
    incoming = jnp.concatenate(
        [before_ref[32:48], g_ref[...], after_ref[32:48]], axis=0
    ).astype(F32)
    hidden = (incoming * gate * (1.0 + pre * (1.0 - gate))).astype(BF16).astype(F32)
    hs[...] = hidden
    total = jnp.zeros((frames, LANES), F32)
    for j in range(KERNEL):
        total = total + w_ref[j : j + 1, :] * hs[31 - j : 31 - j + frames]
    dx_ref[...] = total.astype(BF16)
    centre = hidden[16 : 16 + frames]
    for j in range(KERNEL):
        product = xs[j + 17 : j + 17 + frames] * centre
        dw_ref[j : j + 1, :] = jnp.sum(product, axis=0, keepdims=True)
    dw_ref[KERNEL:, :] = jnp.zeros((1, LANES), F32)


def convolve(x, g, before, after, weight):
    frames, channels = x.shape
    block = lambda rows: pl.BlockSpec((rows, LANES), lambda p: (0, p))
    return pl.pallas_call(
        conv_kernel,
        grid=(channels // LANES,),
        in_specs=[block(frames), block(frames), block(48), block(48), block(KERNEL)],
        out_specs=[block(frames), block(frames), block(KERNEL + 1)],
        out_shape=[
            jax.ShapeDtypeStruct((frames, channels), BF16),
            jax.ShapeDtypeStruct((frames, channels), BF16),
            jax.ShapeDtypeStruct((KERNEL + 1, channels), F32),
        ],
        scratch_shapes=[pltpu.VMEM((frames + 64, LANES), F32), pltpu.VMEM((frames + 32, LANES), F32)],
        compiler_params=pltpu.CompilerParams(dimension_semantics=("arbitrary",)),
        cost_estimate=pl.CostEstimate(
            flops=20_000_000, bytes_accessed=1_000_000, transcendentals=120_000
        ),
        name="conv",
    )(x, g, before, after, weight)


def body(queries, keys, values, out_grad, picks, conv_in, conv_weight, conv_grad):
    me = lax.axis_index("ctx")
    core = me % CORES
    my_x = (me // CORES) % X
    my_z = me // (CORES * X)
    frames = queries.shape[1]

    table = lax.all_gather(jnp.stack([keys[0], values[0]]), "ctx")
    flip = core == 1
    packed = jnp.stack([queries[0], out_grad[0]])
    first, second = packed[:, :, :HALF_INNER], packed[:, :, HALF_INNER:]
    taken = swap_cores(jnp.where(flip, first, second))
    chip = jnp.concatenate([jnp.where(flip, second, first), taken], axis=1)
    slots = jnp.concatenate([picks[0], swap_cores(picks[0])], axis=0)

    ends = CHIPS * CORES - 1
    tail = jnp.concatenate([conv_in[0, frames - 32 :], conv_grad[0, frames - 16 :]], axis=0)
    head = jnp.concatenate([conv_in[0, :32], conv_grad[0, :16]], axis=0)
    before = lax.ppermute(tail, "ctx", [(i, i + 1) for i in range(ends)])
    behind = lax.ppermute(head, "ctx", [(i + 1, i) for i in range(ends)])
    conv_out, conv_dx, partial = convolve(conv_in[0], conv_grad[0], before, behind, conv_weight)

    total = partial + swap_cores(partial)
    total = total + lax.ppermute(total, "dp", [(i, i ^ 1) for i in range(4)])
    total = total + lax.ppermute(total, "dp", [(i, i ^ 2) for i in range(4)])

    attended, query_grad, key_parts, value_parts = attention(
        slots, jnp.stack([my_z, my_x, core]), chip[0], chip[1], total, table
    )

    key_parts = key_parts.reshape(Z, X, SENT, HALF_INNER)
    value_parts = value_parts.reshape(X, Z, ROWS, HALF_INNER)
    key_sum = lax.psum_scatter(
        key_parts, "ctx", scatter_dimension=0, axis_index_groups=COLUMNS
    )
    key_near = [move(key_sum[1], "x", 1), move(key_sum[2], "x", 2), move(key_sum[3], "x", -1)]
    value_sum = scatter_ring([value_parts[d, :, : ROWS - TAIL] for d in range(X)], "x", 0).astype(BF16)
    value_sum = scatter_ring([value_sum[d] for d in range(Z)], "z", 0, [key_sum]).astype(BF16)
    key_sum = key_sum[0].astype(F32) + sum(near.astype(F32) for near in key_near)
    key_total = key_sum[:ROWS].astype(BF16)
    value_total = jnp.concatenate([value_sum, key_sum[ROWS + EXTRA :].astype(BF16)], axis=0)
    weight_grad = key_sum[ROWS : ROWS + WIDTH, :KERNEL].T / math.sqrt(
        conv_in.shape[0] * lax.axis_size("dp") * frames * CHIPS * CORES
    )

    def whole(own, siblings):
        other = swap_cores(siblings)
        return jnp.concatenate([jnp.where(flip, other, own), jnp.where(flip, own, other)], axis=2)

    early = jnp.stack([attended, query_grad])
    early = whole(early[:, :frames], early[:, frames:])
    late = jnp.stack([key_total, value_total])
    lower, upper = late[:, :frames], late[:, frames:]
    late = whole(jnp.where(flip, upper, lower), jnp.where(flip, lower, upper))
    return (
        early[0][None],
        early[1][None],
        late[0][None],
        late[1][None],
        conv_out[None],
        conv_dx[None],
        weight_grad,
    )


def solution(mesh):
    rows = P("dp", "ctx", None)
    return jax.shard_map(
        body,
        mesh=mesh,
        in_specs=(rows, rows, rows, rows, rows, rows, P(), rows),
        out_specs=(rows, rows, rows, rows, rows, rows, P(None, "ctx")),
        check_vma=False,
    )
```

```python
import functools
import math

import jax
import jax.numpy as jnp
from jax import lax
from jax.experimental import pallas as pl
from jax.experimental.pallas import tpu as pltpu
from jax.sharding import PartitionSpec as P

Z, X, CORES = 8, 4, 2
CHIPS = Z * X
BLOCK = 64
HEAD_DIM = 64
LANES = 128
SEL = 16
KERNEL = 31
ROWS = 4 * BLOCK
HALF_INNER = 384
PAIRS = HALF_INNER // LANES
EXTRA = 16
FIRST = 3
GATHERED = [(0, 0), (1, 0), (0, 1), (1, 1)]
PASSED = [(0, 2), (1, 2)]
TAPS = KERNEL + 1
CHANNELS = 768
WIDTH = CHANNELS // (Z * X * CORES)
TAIL = 32
KEPT = ROWS - TAIL
SENT = ROWS + EXTRA + TAIL
F32, BF16 = jnp.float32, jnp.bfloat16


def index_of(z, x, core):
    return (z * X + x) * CORES + core


PLACES = [(z, x, c) for z in range(Z) for x in range(X) for c in range(CORES)]


def along(axis, shift):
    if axis == "z":
        return [(index_of(z, x, c), index_of((z + shift) % Z, x, c)) for z, x, c in PLACES]
    return [(index_of(z, x, c), index_of(z, (x + shift) % X, c)) for z, x, c in PLACES]


def move(value, axis, shift):
    return lax.ppermute(value, "ctx", along(axis, shift))


COLUMNS = [[index_of(z, x, c) for z in range(Z)] for x in range(X) for c in range(CORES)]


def after(value, *others):
    return lax.optimization_barrier((value, *others))[0]


def swap_cores(value):
    return lax.ppermute(value, "ctx", [(i, i ^ 1) for i in range(CHIPS * CORES)])


def plus(a, b):
    return (a.astype(F32) + b.astype(F32)).astype(BF16)


def gather_steps(block, axis, count, dim):
    half = block.shape[dim] // 2
    up = down = block
    for step in range(count // 2):
        if step == count // 2 - 1:
            up = lax.slice_in_dim(up, 0, half, axis=dim)
            down = lax.slice_in_dim(down, half, 2 * half, axis=dim)
        up, down = move(up, axis, 1), move(down, axis, -1)
        wait = yield up, down
        if wait:
            up, down = lax.optimization_barrier((up, down, *wait))[:2]


def in_order(block, arrivals):
    ups, downs = zip(*arrivals)
    return [block, *downs[:-1], ups[-1], downs[-1], *ups[-2::-1]]


def scatter_ring(parts, axis, last=()):
    count = len(parts)
    middle = count // 2
    half = parts[0].shape[-2] // 2

    def low(v):
        return v[..., :half, :]

    def high(v):
        return v[..., half:, :]

    up, down = move(low(parts[middle]), axis, 1), move(high(parts[middle]), axis, -1)
    above, below = parts[middle - 1], parts[middle + 1]
    up = jnp.concatenate([plus(low(above), up), high(above)], axis=-2)
    down = jnp.concatenate([low(below), plus(high(below), down)], axis=-2)
    for d in range(middle - 1, 0, -1):
        if d == 1 and last:
            up, down = after(up, *last), after(down, *last)
        up, down = move(up, axis, 1), move(down, axis, -1)
        if d > 1:
            up, down = plus(up, parts[d - 1]), plus(down, parts[count - d + 1])
    return parts[0].astype(F32) + up.astype(F32) + down.astype(F32)


PIECES = [[(z, x) for z in range(Z)] for x in range(X // 2)]
PIECES += [[(z, X // 2) for z in range(Z // 2)], [(z, X // 2) for z in range(Z // 2, Z)]]
PIECES += [[(z, x) for z in range(Z)] for x in range(X // 2 + 1, X)]


def attention_kernel(
    slots, key_homes, value_homes, place, q_ref, g_ref, total_ref, table_ref, *refs
):
    *pieces, o_ref, dq_ref, dk_ref, dv_ref, pairs, dk, taps, sems = refs
    pair = pl.program_id(0)

    def gathered(which, p, group):
        lanes = pl.ds(pl.multiple_of(place[2] * LANES, LANES), LANES)
        return pltpu.make_async_copy(
            table_ref.at[:, group, :, lanes],
            pairs.at[p, :, :, pl.ds(which * LANES, LANES)],
            sems.at[p, which],
        )

    def passed(which, p, group):
        jobs = []
        for piece, places in zip(pieces, PIECES):
            for i, (dz, dx) in enumerate(places):
                chip = lax.rem(place[0] + dz, Z) * X + lax.rem(place[1] + dx, X)
                jobs.append(
                    pltpu.make_async_copy(
                        piece.at[i, group],
                        pairs.at[p, pl.ds(chip * CORES, CORES), :, pl.ds(which * LANES, LANES)],
                        sems.at[p, which],
                    )
                )
        return jobs

    def copies(p):
        jobs = [gathered(w, q, i) for i, (w, q) in enumerate(GATHERED) if q == p]
        for i, (w, q) in enumerate(PASSED):
            if q == p:
                jobs += passed(w, q, i)
        return jobs

    @pl.when(pair == 0)
    def _():
        for p in range(PAIRS):
            for job in copies(p):
                job.start()

    dk[...] = jnp.zeros_like(dk)
    dv_ref[...] = jnp.zeros_like(dv_ref)

    for p in range(PAIRS):

        @pl.when(pair == p)
        def _(p=p):
            for job in copies(p):
                job.wait()

    left = lax.broadcasted_iota(jnp.int32, (BLOCK, LANES), 1) < HEAD_DIM
    none = jnp.zeros((LANES, LANES), BF16)

    def spread(v):
        zero = jnp.zeros_like(v)
        return jnp.concatenate([jnp.where(left, v, zero), jnp.where(left, zero, v)], axis=0)

    def merge(v):
        return jnp.where(left, v[:BLOCK], v[BLOCK:])

    def dot(a, b, dims):
        return lax.dot_general(a, b, dims, preferred_element_type=F32)

    def add(ref, home, part):
        at = (home // 4, pl.ds(pl.multiple_of(home % 4 * BLOCK, BLOCK), BLOCK), slice(None))
        ref[at] = (ref[at].astype(F32) + part).astype(BF16)

    scale = 1.0 / math.sqrt(HEAD_DIM)

    def visit(b):
        rows = slice(b * BLOCK, (b + 1) * BLOCK)
        both = jnp.concatenate(
            [
                pairs[
                    pair,
                    slots[b, j] // 2,
                    pl.ds(pl.multiple_of(slots[b, j] % 2 * BLOCK, BLOCK), BLOCK),
                    :,
                ]
                for j in range(SEL)
            ],
            axis=0,
        )
        query = spread((q_ref[rows, :].astype(F32) * scale).astype(BF16))
        grad = spread(g_ref[rows, :])
        sides = jnp.concatenate(
            [jnp.concatenate([query, none], axis=1), jnp.concatenate([none, grad], axis=1)], axis=0
        )
        products = dot(both, sides, (((1,), (1,)), ((), ())))
        scores, prob_grad = products[:, :LANES], products[:, LANES:]
        scores = jnp.exp(scores - jnp.max(scores, axis=0, keepdims=True))
        probs = scores * (1.0 / jnp.sum(scores, axis=0, keepdims=True))
        delta = jnp.sum(probs * prob_grad, axis=0, keepdims=True)
        slope = probs * (prob_grad - delta)
        factors = jnp.concatenate([slope.astype(BF16), probs.astype(BF16)], axis=1)
        sums = dot(factors, both, (((0,), (0,)), ((), ())))
        dq_ref[rows, :] = (merge(sums[:LANES, :LANES]) * scale).astype(BF16)
        o_ref[rows, :] = merge(sums[LANES:, LANES:]).astype(BF16)
        parts = dot(factors, sides, (((1,), (0,)), ((), ())))
        for j in range(SEL):
            part = slice(j * BLOCK, (j + 1) * BLOCK)
            add(dk, key_homes[b, j], parts[part, :LANES])
            add(dv_ref, value_homes[b, j], parts[part, LANES:])

    for b in range(4):
        visit(b)

    for i in range(CHIPS):
        dk_ref[i] = dk[i, :KEPT, :]
        z, x = lax.rem(i % Z + FIRST + place[0], Z), i // Z
        dv_ref[i, ROWS + EXTRA :, :] = dk[z * X + x, KEPT:, :]

    @pl.when(pair == 0)
    def _():
        for c in range(CHANNELS // LANES):
            part = slice(c * LANES, (c + 1) * LANES)
            taps[part] = total_ref[:, part].T
        odd = place[2] == 1
        blank = jnp.zeros((EXTRA, LANES - TAPS), F32)
        fill = jnp.zeros((EXTRA - WIDTH, TAPS), F32)

        def extra(i, carry):
            z, x = lax.rem(i % Z + FIRST + place[0], Z), lax.rem(i // Z + place[1], X)
            chip = z * X + x
            both = taps[pl.ds(pl.multiple_of(chip * 2 * WIDTH, 2 * WIDTH), 2 * WIDTH)]
            mine = jnp.where(odd, both[WIDTH:], both[:WIDTH])
            mine = jnp.concatenate([jnp.concatenate([mine, fill], axis=0), blank], axis=1)
            dv_ref[i, pl.ds(ROWS, EXTRA), :] = mine.astype(BF16)
            return carry

        lax.fori_loop(0, CHIPS, extra, 0)


def attention(slots, place, queries, grads, total, table, pieces):
    owner = slots // 2
    z, x = owner // (CORES * X), owner // CORES % X
    dz, dx = (z - place[0]) % Z, (x - place[1]) % X
    inner = owner % CORES * 2 + slots % 2
    key_homes = (z * X + dx) * 4 + inner
    value_homes = (dx * Z + (dz + Z - FIRST) % Z) * 4 + inner
    lane_block = lambda rows: pl.BlockSpec((rows, LANES), lambda p, *_: (0, p))
    chip_block = lambda rows: pl.BlockSpec((CHIPS, rows, LANES), lambda p, *_: (0, 0, p))
    return pl.pallas_call(
        attention_kernel,
        grid_spec=pltpu.PrefetchScalarGridSpec(
            num_scalar_prefetch=4,
            grid=(PAIRS,),
            in_specs=[
                lane_block(ROWS),
                lane_block(ROWS),
                pl.BlockSpec((TAPS, CHANNELS), lambda p, *_: (0, 0)),
            ]
            + [pl.BlockSpec(memory_space=pl.ANY)] * (1 + len(pieces)),
            out_specs=[
                lane_block(ROWS),
                lane_block(ROWS),
                chip_block(KEPT),
                chip_block(SENT),
            ],
            scratch_shapes=[
                pltpu.VMEM((PAIRS, CHIPS * CORES, ROWS // CORES, 2 * LANES), BF16),
                pltpu.VMEM((CHIPS, ROWS, LANES), BF16),
                pltpu.VMEM((CHANNELS, TAPS), F32),
                pltpu.SemaphoreType.DMA((PAIRS, 2)),
            ],
        ),
        out_shape=[
            jax.ShapeDtypeStruct((ROWS, HALF_INNER), BF16),
            jax.ShapeDtypeStruct((ROWS, HALF_INNER), BF16),
            jax.ShapeDtypeStruct((CHIPS, KEPT, HALF_INNER), BF16),
            jax.ShapeDtypeStruct((CHIPS, SENT, HALF_INNER), BF16),
        ],
        compiler_params=pltpu.CompilerParams(
            dimension_semantics=("arbitrary",), vmem_limit_bytes=50 * 1024 * 1024
        ),
        cost_estimate=pl.CostEstimate(
            flops=2_400_000_000, bytes_accessed=26_000_000, transcendentals=1_600_000
        ),
        name="attend",
    )(slots, key_homes, value_homes, place, queries, grads, total, table, *pieces)


def conv_kernel(x_ref, g_ref, before_ref, after_ref, w_ref, out_ref, dx_ref, dw_ref, xs, hs):
    frames = x_ref.shape[0]
    xs[0:32] = before_ref[0:32].astype(F32)
    xs[32 : 32 + frames] = x_ref[...].astype(F32)
    xs[32 + frames : 64 + frames] = after_ref[0:32].astype(F32)
    wide = frames + 32
    pre = jnp.zeros((wide, LANES), F32)
    for j in range(KERNEL):
        pre = pre + w_ref[j : j + 1, :] * xs[j + 1 : j + 1 + wide]
    gate = 1.0 / (1.0 + jnp.exp(-pre))
    out_ref[...] = (pre * gate)[16 : 16 + frames].astype(BF16)
    incoming = jnp.concatenate(
        [before_ref[32:48], g_ref[...], after_ref[32:48]], axis=0
    ).astype(F32)
    hidden = (incoming * gate * (1.0 + pre * (1.0 - gate))).astype(BF16).astype(F32)
    hs[...] = hidden
    total = jnp.zeros((frames, LANES), F32)
    for j in range(KERNEL):
        total = total + w_ref[j : j + 1, :] * hs[31 - j : 31 - j + frames]
    dx_ref[...] = total.astype(BF16)
    centre = hidden[16 : 16 + frames]
    for j in range(KERNEL):
        product = xs[j + 17 : j + 17 + frames] * centre
        dw_ref[j : j + 1, :] = jnp.sum(product, axis=0, keepdims=True)
    dw_ref[KERNEL:, :] = jnp.zeros((1, LANES), F32)


def convolve(x, g, before, after, weight):
    frames, channels = x.shape
    block = lambda rows: pl.BlockSpec((rows, LANES), lambda p: (0, p))
    return pl.pallas_call(
        conv_kernel,
        grid=(channels // LANES,),
        in_specs=[block(frames), block(frames), block(48), block(48), block(KERNEL)],
        out_specs=[block(frames), block(frames), block(KERNEL + 1)],
        out_shape=[
            jax.ShapeDtypeStruct((frames, channels), BF16),
            jax.ShapeDtypeStruct((frames, channels), BF16),
            jax.ShapeDtypeStruct((KERNEL + 1, channels), F32),
        ],
        scratch_shapes=[pltpu.VMEM((frames + 64, LANES), F32), pltpu.VMEM((frames + 32, LANES), F32)],
        compiler_params=pltpu.CompilerParams(dimension_semantics=("arbitrary",)),
        cost_estimate=pl.CostEstimate(
            flops=20_000_000, bytes_accessed=1_000_000, transcendentals=120_000
        ),
        name="conv",
    )(x, g, before, after, weight)


def body(queries, keys, values, out_grad, picks, conv_in, conv_weight, conv_grad):
    me = lax.axis_index("ctx")
    core = me % CORES
    my_x = (me // CORES) % X
    my_z = me // (CORES * X)
    frames = queries.shape[1]

    def lanes(which, p, side):
        start = side * HALF_INNER + p * LANES
        return (keys, values)[which][0, :, start : start + LANES]

    table = lax.all_gather(
        jnp.stack([jnp.concatenate([lanes(w, p, 0), lanes(w, p, 1)], axis=1) for w, p in GATHERED]),
        "ctx",
    )
    flip = core == 1
    sides = [jnp.stack([lanes(w, p, side) for w, p in PASSED]) for side in range(CORES)]
    mine = jnp.where(flip, sides[1], sides[0])
    taken = swap_cores(jnp.where(flip, sides[0], sides[1]))
    block = jnp.stack([jnp.where(flip, taken, mine), jnp.where(flip, mine, taken)], axis=1)
    steps = gather_steps(block[None], "z", Z, 2)
    column = [next(steps)]
    for _ in range(Z // 2 - 1):
        column.append(steps.send(None))
    column = in_order(block[None], column)
    middle = Z // 2
    column[middle : middle + 2] = [jnp.concatenate(column[middle : middle + 2], axis=2)]
    column = jnp.concatenate(column)
    steps = gather_steps(column, "x", X, 0)
    pieces = [next(steps)]
    for _ in range(X // 2 - 1):
        pieces.append(steps.send(None))
    pieces = in_order(column, pieces)

    packed = jnp.stack([queries[0], out_grad[0]])
    first, second = packed[:, :, :HALF_INNER], packed[:, :, HALF_INNER:]
    taken = swap_cores(jnp.where(flip, first, second))
    chip = jnp.concatenate([jnp.where(flip, second, first), taken], axis=1)
    slots = jnp.concatenate([picks[0], swap_cores(picks[0])], axis=0)

    ends = CHIPS * CORES - 1
    tail = jnp.concatenate([conv_in[0, frames - 32 :], conv_grad[0, frames - 16 :]], axis=0)
    head = jnp.concatenate([conv_in[0, :32], conv_grad[0, :16]], axis=0)
    before = lax.ppermute(tail, "ctx", [(i, i + 1) for i in range(ends)])
    behind = lax.ppermute(head, "ctx", [(i + 1, i) for i in range(ends)])
    conv_out, conv_dx, partial = convolve(conv_in[0], conv_grad[0], before, behind, conv_weight)

    total = partial + swap_cores(partial)
    total = total + lax.ppermute(total, "dp", [(i, i ^ 1) for i in range(4)])
    total = total + lax.ppermute(total, "dp", [(i, i ^ 2) for i in range(4)])

    attended, query_grad, key_parts, value_parts = attention(
        slots, jnp.stack([my_z, my_x, core]), chip[0], chip[1], total, table, pieces
    )

    key_parts = key_parts.reshape(Z, X, KEPT, HALF_INNER)
    value_parts = value_parts.reshape(X, Z, SENT, HALF_INNER)
    key_sum = lax.psum_scatter(
        key_parts, "ctx", scatter_dimension=0, axis_index_groups=COLUMNS
    )
    key_near = [move(key_sum[1], "x", 1), move(key_sum[2], "x", 2), move(key_sum[3], "x", -1)]
    early = scatter_ring([value_parts[d, :FIRST] for d in range(X)], "x").astype(BF16)
    late = scatter_ring([value_parts[d, FIRST:] for d in range(X)], "x").astype(BF16)
    by_z = [early[d] for d in range(FIRST)] + [late[d] for d in range(Z - FIRST)]
    value_sum = scatter_ring([by_z[(d + Z - FIRST) % Z] for d in range(Z)], "z", (key_sum,))
    key_sum = key_sum[0].astype(F32) + sum(near.astype(F32) for near in key_near)
    key_total = jnp.concatenate([key_sum, value_sum[ROWS + EXTRA :]]).astype(BF16)
    value_total = value_sum[:ROWS].astype(BF16)
    weight_grad = value_sum[ROWS : ROWS + WIDTH, :KERNEL].T / math.sqrt(
        conv_in.shape[0] * lax.axis_size("dp") * frames * CHIPS * CORES
    )

    def whole(own, siblings):
        other = swap_cores(siblings)
        return jnp.concatenate([jnp.where(flip, other, own), jnp.where(flip, own, other)], axis=2)

    early = jnp.stack([attended, query_grad])
    early = whole(early[:, :frames], early[:, frames:])
    late = jnp.stack([key_total, value_total])
    lower, upper = late[:, :frames], late[:, frames:]
    late = whole(jnp.where(flip, upper, lower), jnp.where(flip, lower, upper))
    return (
        early[0][None],
        early[1][None],
        late[0][None],
        late[1][None],
        conv_out[None],
        conv_dx[None],
        weight_grad,
    )


def solution(mesh):
    rows = P("dp", "ctx", None)
    return jax.shard_map(
        body,
        mesh=mesh,
        in_specs=(rows, rows, rows, rows, rows, rows, P(), rows),
        out_specs=(rows, rows, rows, rows, rows, rows, P(None, "ctx")),
        check_vma=False,
    )
```

```python
import functools
import math

import jax
import jax.numpy as jnp
from jax import lax
from jax.experimental import pallas as pl
from jax.experimental.pallas import tpu as pltpu
from jax.sharding import PartitionSpec as P

Z, X, CORES = 8, 4, 2
CHIPS = Z * X
BLOCK = 64
HEAD_DIM = 64
LANES = 128
SEL = 16
KERNEL = 31
ROWS = 4 * BLOCK
HALF_INNER = 384
PAIRS = HALF_INNER // LANES
EXTRA = 16
CHUNK = 256
FIRST = 3
GATHERED = [(0, 0), (1, 0), (0, 1), (1, 1)]
PASSED = [(0, 2), (1, 2)]
TABLE, RING = (0, 1), (2,)
TAPS = KERNEL + 1
CHANNELS = 768
WIDTH = CHANNELS // (Z * X * CORES)
TAIL = 32
KEPT = ROWS - TAIL
SENT = ROWS + EXTRA + TAIL
F32, BF16 = jnp.float32, jnp.bfloat16


def index_of(z, x, core):
    return (z * X + x) * CORES + core


PLACES = [(z, x, c) for z in range(Z) for x in range(X) for c in range(CORES)]


def along(axis, shift):
    if axis == "z":
        return [(index_of(z, x, c), index_of((z + shift) % Z, x, c)) for z, x, c in PLACES]
    return [(index_of(z, x, c), index_of(z, (x + shift) % X, c)) for z, x, c in PLACES]


def move(value, axis, shift):
    return lax.ppermute(value, "ctx", along(axis, shift))


COLUMNS = [[index_of(z, x, c) for z in range(Z)] for x in range(X) for c in range(CORES)]


def after(value, *others):
    return lax.optimization_barrier((value, *others))[0]


def swap_cores(value):
    return lax.ppermute(value, "ctx", [(i, i ^ 1) for i in range(CHIPS * CORES)])


def plus(a, b):
    return (a.astype(F32) + b.astype(F32)).astype(BF16)


def scatter_across(parts, far_up, far_down):
    cut = far_up.shape[0]
    above, below = parts[1], parts[3]
    up, down = move(far_up, "x", 1), move(far_down, "x", -1)
    up = jnp.concatenate([plus(above[:cut], up), above[cut:]])
    down = jnp.concatenate([below[:cut], plus(below[cut:], down)])
    up, down = move(up, "x", 1), move(down, "x", -1)
    return parts[0].astype(F32) + up.astype(F32) + down.astype(F32)


def gather_steps(block, axis, count, dim):
    half = block.shape[dim] // 2
    up = down = block
    for step in range(count // 2):
        if step == count // 2 - 1:
            up = lax.slice_in_dim(up, 0, half, axis=dim)
            down = lax.slice_in_dim(down, half, 2 * half, axis=dim)
        up, down = move(up, axis, 1), move(down, axis, -1)
        wait = yield up, down
        if wait:
            up, down = lax.optimization_barrier((up, down, *wait))[:2]


def in_order(block, arrivals):
    ups, downs = zip(*arrivals)
    return [block, *downs[:-1], ups[-1], downs[-1], *ups[-2::-1]]


def scatter_ring(parts, axis, last=()):
    count = len(parts)
    middle = count // 2
    half = parts[0].shape[-2] // 2

    def low(v):
        return v[..., :half, :]

    def high(v):
        return v[..., half:, :]

    up, down = move(low(parts[middle]), axis, 1), move(high(parts[middle]), axis, -1)
    above, below = parts[middle - 1], parts[middle + 1]
    up = jnp.concatenate([plus(low(above), up), high(above)], axis=-2)
    down = jnp.concatenate([low(below), plus(high(below), down)], axis=-2)
    for d in range(middle - 1, 0, -1):
        if d == 1 and last:
            up, down = after(up, *last), after(down, *last)
        up, down = move(up, axis, 1), move(down, axis, -1)
        if d > 1:
            up, down = plus(up, parts[d - 1]), plus(down, parts[count - d + 1])
    return parts[0].astype(F32) + up.astype(F32) + down.astype(F32)


PIECES = [[(z, x) for z in range(Z)] for x in range(X // 2)]
PIECES += [[(z, X // 2) for z in range(Z // 2)], [(z, X // 2) for z in range(Z // 2, Z)]]
PIECES += [[(z, x) for z in range(Z)] for x in range(X // 2 + 1, X)]


FAR = [(0, 1), (1, 3), (3, 6), (6, 8)]
RESULTS = 4 + len(FAR)


def attention_kernel(mine, slots, key_homes, value_homes, place, q_ref, g_ref, *refs):
    if mine == RING:
        *pieces, pairs, dk, work, sems = refs
        pieces, results = pieces[:-RESULTS], pieces[-RESULTS:]
    else:
        total_ref, table_ref, *results, pairs, dk, work, taps, sems = refs
        results = results[RESULTS:]
    o_ref, dq_ref, dk_ref, dv_ref, *far_refs = results
    pair = pl.program_id(0)

    def gathered(which, p, group):
        lanes = pl.ds(pl.multiple_of(place[2] * LANES, LANES), LANES)
        return pltpu.make_async_copy(
            table_ref.at[:, group, :, lanes],
            pairs.at[p, :, :, pl.ds(which * LANES, LANES)],
            sems.at[p, which],
        )

    def passed(which, p, group):
        jobs = []
        for piece, places in zip(pieces, PIECES):
            for i, (dz, dx) in enumerate(places):
                chip = lax.rem(place[0] + dz, Z) * X + lax.rem(place[1] + dx, X)
                jobs.append(
                    pltpu.make_async_copy(
                        piece.at[i, group],
                        pairs.at[p, pl.ds(chip * CORES, CORES), :, pl.ds(which * LANES, LANES)],
                        sems.at[p, which],
                    )
                )
        return jobs

    def copies(p):
        jobs = [gathered(w, p, i) for i, (w, q) in enumerate(GATHERED) if q == mine[p]]
        for i, (w, q) in enumerate(PASSED):
            if q == mine[p]:
                jobs += passed(w, p, i)
        return jobs

    @pl.when(pair == 0)
    def _():
        for p in range(len(mine)):
            for job in copies(p):
                job.start()

    dk[...] = jnp.zeros_like(dk)
    dv_ref[...] = jnp.zeros_like(dv_ref)

    for p in range(len(mine)):

        @pl.when(pair == p)
        def _(p=p):
            for job in copies(p):
                job.wait()

    left = lax.broadcasted_iota(jnp.int32, (BLOCK, LANES), 1) < HEAD_DIM
    none = jnp.zeros((LANES, LANES), BF16)

    def spread(v):
        zero = jnp.zeros_like(v)
        return jnp.concatenate([jnp.where(left, v, zero), jnp.where(left, zero, v)], axis=0)

    def merge(v):
        return jnp.where(left, v[:BLOCK], v[BLOCK:])

    def dot(a, b, dims):
        return lax.dot_general(a, b, dims, preferred_element_type=F32)

    def add(ref, home, part):
        at = (home // 4, pl.ds(pl.multiple_of(home % 4 * BLOCK, BLOCK), BLOCK), slice(None))
        ref[at] = (ref[at].astype(F32) + part).astype(BF16)

    scale = 1.0 / math.sqrt(HEAD_DIM)

    def visit(b):
        rows = slice(b * BLOCK, (b + 1) * BLOCK)
        both = jnp.concatenate(
            [
                pairs[
                    pair,
                    slots[b, j] // 2,
                    pl.ds(pl.multiple_of(slots[b, j] % 2 * BLOCK, BLOCK), BLOCK),
                    :,
                ]
                for j in range(SEL)
            ],
            axis=0,
        )
        query = spread((q_ref[rows, :].astype(F32) * scale).astype(BF16))
        grad = spread(g_ref[rows, :])
        sides = jnp.concatenate(
            [jnp.concatenate([query, none], axis=1), jnp.concatenate([none, grad], axis=1)], axis=0
        )
        chunks = [slice(c, c + CHUNK) for c in range(0, SEL * BLOCK, CHUNK)]
        keys_here, values_here = slice(0, LANES), slice(LANES, 2 * LANES)
        room = work.at[b % 2]
        top = None
        for c in chunks:
            products = dot(both[c], sides, (((1,), (1,)), ((), ())))
            room[c, :] = products
            highest = jnp.max(products[:, keys_here], axis=0, keepdims=True)
            top = highest if top is None else jnp.maximum(top, highest)
        mass = moment = 0.0
        for c in chunks:
            scores = jnp.exp(room[c, keys_here] - top)
            room[c, keys_here] = scores
            mass = mass + jnp.sum(scores, axis=0, keepdims=True)
            moment = moment + jnp.sum(scores * room[c, values_here], axis=0, keepdims=True)
        inverse = 1.0 / mass
        delta = moment * inverse
        sums = 0.0
        for c in chunks:
            probs = room[c, keys_here] * inverse
            slope = probs * (room[c, values_here] - delta)
            factors = jnp.concatenate([slope.astype(BF16), probs.astype(BF16)], axis=1)
            sums = sums + dot(factors, both[c], (((0,), (0,)), ((), ())))
            parts = dot(factors, sides, (((1,), (0,)), ((), ())))
            for i in range(CHUNK // BLOCK):
                part = slice(i * BLOCK, (i + 1) * BLOCK)
                j = c.start // BLOCK + i
                add(dk, key_homes[b, j], parts[part, :LANES])
                add(dv_ref, value_homes[b, j], parts[part, LANES:])
        dq_ref[rows, :] = (merge(sums[:LANES, :LANES]) * scale).astype(BF16)
        o_ref[rows, :] = merge(sums[LANES:, LANES:]).astype(BF16)

    for b in range(4):
        visit(b)

    for i in range(CHIPS):
        dk_ref[i] = dk[i, :KEPT, :]
        z, x = lax.rem(i % Z + FIRST + place[0], Z), i // Z
        dv_ref[i, ROWS + EXTRA :, :] = dk[z * X + x, KEPT:, :]

    if mine != RING:
        @pl.when(pair == 0)
        def _():
            for c in range(CHANNELS // LANES):
                part = slice(c * LANES, (c + 1) * LANES)
                taps[part] = total_ref[:, part].T
            odd = place[2] == 1
            blank = jnp.zeros((EXTRA, LANES - TAPS), F32)
            fill = jnp.zeros((EXTRA - WIDTH, TAPS), F32)

            def extra(i, carry):
                z, x = lax.rem(i % Z + FIRST + place[0], Z), lax.rem(i // Z + place[1], X)
                chip = z * X + x
                both = taps[pl.ds(pl.multiple_of(chip * 2 * WIDTH, 2 * WIDTH), 2 * WIDTH)]
                mine = jnp.where(odd, both[WIDTH:], both[:WIDTH])
                mine = jnp.concatenate([jnp.concatenate([mine, fill], axis=0), blank], axis=1)
                dv_ref[i, pl.ds(ROWS, EXTRA), :] = mine.astype(BF16)
                return carry

            lax.fori_loop(0, CHIPS, extra, 0)

    for ref, (first, end) in zip(far_refs, FAR):
        for i in range(first, end):
            ref[i - first] = dv_ref[X // 2 * Z + i]


def attention(slots, place, queries, grads, total, table, pieces):
    owner = slots // 2
    z, x = owner // (CORES * X), owner // CORES % X
    dz, dx = (z - place[0]) % Z, (x - place[1]) % X
    inner = owner % CORES * 2 + slots % 2
    key_homes = (z * X + dx) * 4 + inner
    value_homes = (dx * Z + (dz + Z - FIRST) % Z) * 4 + inner
    scalars = (slots, key_homes, value_homes, place)
    any_space = pl.BlockSpec(memory_space=pl.ANY)

    def call(mine, more, specs, held, scratch):
        lane_block = lambda rows: pl.BlockSpec((rows, LANES), lambda p, *_: (0, p + mine[0]))
        chip_block = lambda chips, rows: pl.BlockSpec(
            (chips, rows, LANES), lambda p, *_: (0, 0, p + mine[0])
        )
        shapes = [(ROWS,), (ROWS,), (CHIPS, KEPT), (CHIPS, SENT)]
        shapes += [(end - first, SENT) for first, end in FAR]
        inputs = (*scalars, queries, grads, *more)
        return pl.pallas_call(
            functools.partial(attention_kernel, mine),
            grid_spec=pltpu.PrefetchScalarGridSpec(
                num_scalar_prefetch=len(scalars),
                grid=(len(mine),),
                in_specs=[lane_block(ROWS), lane_block(ROWS), *specs, *[any_space] * len(held)],
                out_specs=[
                    lane_block(*shape) if len(shape) == 1 else chip_block(*shape) for shape in shapes
                ],
                scratch_shapes=[
                    pltpu.VMEM((len(mine), CHIPS * CORES, ROWS // CORES, 2 * LANES), BF16),
                    pltpu.VMEM((CHIPS, ROWS, LANES), BF16),
                    pltpu.VMEM((2, SEL * BLOCK, 2 * LANES), F32),
                    *scratch,
                    pltpu.SemaphoreType.DMA((len(mine), 2)),
                ],
            ),
            out_shape=[jax.ShapeDtypeStruct((*shape, HALF_INNER), BF16) for shape in shapes],
            input_output_aliases={len(inputs) + i: i for i in range(len(held))},
            compiler_params=pltpu.CompilerParams(
                dimension_semantics=("arbitrary",), vmem_limit_bytes=50 * 1024 * 1024
            ),
            cost_estimate=pl.CostEstimate(
                flops=1_600_000_000 * len(mine),
                bytes_accessed=9_000_000 * len(mine),
                transcendentals=530_000 * len(mine),
            ),
            name="attend",
        )(*inputs, *held)

    held = call(RING, pieces, [any_space] * len(pieces), (), ())
    whole = pl.BlockSpec((TAPS, CHANNELS), lambda p, *_: (0, 0))
    return call(
        TABLE, (total, table), [whole, any_space], held, [pltpu.VMEM((CHANNELS, TAPS), F32)]
    )


def conv_kernel(x_ref, g_ref, before_ref, after_ref, w_ref, out_ref, dx_ref, dw_ref, xs, hs):
    frames = x_ref.shape[0]
    xs[0:32] = before_ref[0:32].astype(F32)
    xs[32 : 32 + frames] = x_ref[...].astype(F32)
    xs[32 + frames : 64 + frames] = after_ref[0:32].astype(F32)
    wide = frames + 32
    pre = jnp.zeros((wide, LANES), F32)
    for j in range(KERNEL):
        pre = pre + w_ref[j : j + 1, :] * xs[j + 1 : j + 1 + wide]
    gate = 1.0 / (1.0 + jnp.exp(-pre))
    out_ref[...] = (pre * gate)[16 : 16 + frames].astype(BF16)
    incoming = jnp.concatenate(
        [before_ref[32:48], g_ref[...], after_ref[32:48]], axis=0
    ).astype(F32)
    hidden = (incoming * gate * (1.0 + pre * (1.0 - gate))).astype(BF16).astype(F32)
    hs[...] = hidden
    total = jnp.zeros((frames, LANES), F32)
    for j in range(KERNEL):
        total = total + w_ref[j : j + 1, :] * hs[31 - j : 31 - j + frames]
    dx_ref[...] = total.astype(BF16)
    centre = hidden[16 : 16 + frames]
    for j in range(KERNEL):
        product = xs[j + 17 : j + 17 + frames] * centre
        dw_ref[j : j + 1, :] = jnp.sum(product, axis=0, keepdims=True)
    dw_ref[KERNEL:, :] = jnp.zeros((1, LANES), F32)


def convolve(x, g, before, after, weight):
    frames, channels = x.shape
    block = lambda rows: pl.BlockSpec((rows, LANES), lambda p: (0, p))
    return pl.pallas_call(
        conv_kernel,
        grid=(channels // LANES,),
        in_specs=[block(frames), block(frames), block(48), block(48), block(KERNEL)],
        out_specs=[block(frames), block(frames), block(KERNEL + 1)],
        out_shape=[
            jax.ShapeDtypeStruct((frames, channels), BF16),
            jax.ShapeDtypeStruct((frames, channels), BF16),
            jax.ShapeDtypeStruct((KERNEL + 1, channels), F32),
        ],
        scratch_shapes=[pltpu.VMEM((frames + 64, LANES), F32), pltpu.VMEM((frames + 32, LANES), F32)],
        compiler_params=pltpu.CompilerParams(dimension_semantics=("arbitrary",)),
        cost_estimate=pl.CostEstimate(
            flops=20_000_000, bytes_accessed=1_000_000, transcendentals=120_000
        ),
        name="conv",
    )(x, g, before, after, weight)


def body(queries, keys, values, out_grad, picks, conv_in, conv_weight, conv_grad):
    me = lax.axis_index("ctx")
    core = me % CORES
    my_x = (me // CORES) % X
    my_z = me // (CORES * X)
    frames = queries.shape[1]

    def lanes(which, p, side):
        start = side * HALF_INNER + p * LANES
        return (keys, values)[which][0, :, start : start + LANES]

    table = lax.all_gather(
        jnp.stack([jnp.concatenate([lanes(w, p, 0), lanes(w, p, 1)], axis=1) for w, p in GATHERED]),
        "ctx",
    )
    flip = core == 1
    sides = [jnp.stack([lanes(w, p, side) for w, p in PASSED]) for side in range(CORES)]
    mine = jnp.where(flip, sides[1], sides[0])
    taken = swap_cores(jnp.where(flip, sides[0], sides[1]))
    block = jnp.stack([jnp.where(flip, taken, mine), jnp.where(flip, mine, taken)], axis=1)
    steps = gather_steps(block[None], "z", Z, 2)
    column = [next(steps)]
    for _ in range(Z // 2 - 1):
        column.append(steps.send(None))
    column = in_order(block[None], column)
    middle = Z // 2
    column[middle : middle + 2] = [jnp.concatenate(column[middle : middle + 2], axis=2)]
    column = jnp.concatenate(column)
    steps = gather_steps(column, "x", X, 0)
    pieces = [next(steps)]
    for _ in range(X // 2 - 1):
        pieces.append(steps.send(None))
    pieces = in_order(column, pieces)

    packed = jnp.stack([queries[0], out_grad[0]])
    first, second = packed[:, :, :HALF_INNER], packed[:, :, HALF_INNER:]
    taken = swap_cores(jnp.where(flip, first, second))
    chip = jnp.concatenate([jnp.where(flip, second, first), taken], axis=1)
    slots = jnp.concatenate([picks[0], swap_cores(picks[0])], axis=0)

    ends = CHIPS * CORES - 1
    tail = jnp.concatenate([conv_in[0, frames - 32 :], conv_grad[0, frames - 16 :]], axis=0)
    head = jnp.concatenate([conv_in[0, :32], conv_grad[0, :16]], axis=0)
    before = lax.ppermute(tail, "ctx", [(i, i + 1) for i in range(ends)])
    behind = lax.ppermute(head, "ctx", [(i + 1, i) for i in range(ends)])
    conv_out, conv_dx, partial = convolve(conv_in[0], conv_grad[0], before, behind, conv_weight)

    total = partial + swap_cores(partial)
    total = total + lax.ppermute(total, "dp", [(i, i ^ 1) for i in range(4)])
    total = total + lax.ppermute(total, "dp", [(i, i ^ 2) for i in range(4)])

    attended, query_grad, key_parts, value_parts, *far_parts = attention(
        slots, jnp.stack([my_z, my_x, core]), chip[0], chip[1], total, table, pieces
    )

    key_parts = key_parts.reshape(Z, X, KEPT, HALF_INNER)
    value_parts = value_parts.reshape(X, Z, SENT, HALF_INNER)
    key_sum = lax.psum_scatter(
        key_parts, "ctx", scatter_dimension=0, axis_index_groups=COLUMNS
    )
    key_near = [move(key_sum[1], "x", 1), move(key_sum[2], "x", 2), move(key_sum[3], "x", -1)]
    early = scatter_across([value_parts[d, :FIRST] for d in range(X)], *far_parts[:2]).astype(BF16)
    late = scatter_across([value_parts[d, FIRST:] for d in range(X)], *far_parts[2:]).astype(BF16)
    by_z = [early[d] for d in range(FIRST)] + [late[d] for d in range(Z - FIRST)]
    value_sum = scatter_ring([by_z[(d + Z - FIRST) % Z] for d in range(Z)], "z", (key_sum,))
    key_sum = key_sum[0].astype(F32) + sum(near.astype(F32) for near in key_near)
    key_total = jnp.concatenate([key_sum, value_sum[ROWS + EXTRA :]]).astype(BF16)
    value_total = value_sum[:ROWS].astype(BF16)
    weight_grad = value_sum[ROWS : ROWS + WIDTH, :KERNEL].T / math.sqrt(
        conv_in.shape[0] * lax.axis_size("dp") * frames * CHIPS * CORES
    )

    def whole(own, siblings):
        other = swap_cores(siblings)
        return jnp.concatenate([jnp.where(flip, other, own), jnp.where(flip, own, other)], axis=2)

    early = jnp.stack([attended, query_grad])
    early = whole(early[:, :frames], early[:, frames:])
    late = jnp.stack([key_total, value_total])
    lower, upper = late[:, :frames], late[:, frames:]
    late = whole(jnp.where(flip, upper, lower), jnp.where(flip, lower, upper))
    return (
        early[0][None],
        early[1][None],
        late[0][None],
        late[1][None],
        conv_out[None],
        conv_dx[None],
        weight_grad,
    )


def solution(mesh):
    rows = P("dp", "ctx", None)
    return jax.shard_map(
        body,
        mesh=mesh,
        in_specs=(rows, rows, rows, rows, rows, rows, P(), rows),
        out_specs=(rows, rows, rows, rows, rows, rows, P(None, "ctx")),
        check_vma=False,
    )
```

```python
import functools
import math

import jax
import jax.numpy as jnp
from jax import lax
from jax.experimental import pallas as pl
from jax.experimental.pallas import tpu as pltpu
from jax.sharding import PartitionSpec as P

Z, X, CORES = 8, 4, 2
CHIPS = Z * X
BLOCK = 64
HEAD_DIM = 64
LANES = 128
SEL = 16
KERNEL = 31
ROWS = 4 * BLOCK
HALF_INNER = 384
PAIRS = HALF_INNER // LANES
EXTRA = 16
CHUNK = 256
FIRST = 3
GATHERED = [(0, 0), (1, 0), (0, 1), (1, 1)]
PASSED = [(0, 2), (1, 2)]
TABLE, RING = (0, 1), (2,)
TAPS = KERNEL + 1
CHANNELS = 768
WIDTH = CHANNELS // (Z * X * CORES)
TAIL = 32
KEPT = ROWS - TAIL
SENT = ROWS + EXTRA + TAIL
F32, BF16 = jnp.float32, jnp.bfloat16


def index_of(z, x, core):
    return (z * X + x) * CORES + core


PLACES = [(z, x, c) for z in range(Z) for x in range(X) for c in range(CORES)]


def along(axis, shift):
    if axis == "z":
        return [(index_of(z, x, c), index_of((z + shift) % Z, x, c)) for z, x, c in PLACES]
    return [(index_of(z, x, c), index_of(z, (x + shift) % X, c)) for z, x, c in PLACES]


def move(value, axis, shift):
    return lax.ppermute(value, "ctx", along(axis, shift))


COLUMNS = [[index_of(z, x, c) for z in range(Z)] for x in range(X) for c in range(CORES)]


def after(value, *others):
    return lax.optimization_barrier((value, *others))[0]


def swap_cores(value):
    return lax.ppermute(value, "ctx", [(i, i ^ 1) for i in range(CHIPS * CORES)])


def plus(a, b):
    return (a.astype(F32) + b.astype(F32)).astype(BF16)


def scatter_across(parts, far_up, far_down):
    cut = far_up.shape[0]
    above, below = parts[1], parts[3]
    up, down = move(far_up, "x", 1), move(far_down, "x", -1)
    up = jnp.concatenate([plus(above[:cut], up), above[cut:]])
    down = jnp.concatenate([below[:cut], plus(below[cut:], down)])
    up, down = move(up, "x", 1), move(down, "x", -1)
    return parts[0].astype(F32) + up.astype(F32) + down.astype(F32)


def gather_steps(block, axis, count, dim):
    half = block.shape[dim] // 2
    up = down = block
    for step in range(count // 2):
        if step == count // 2 - 1:
            up = lax.slice_in_dim(up, 0, half, axis=dim)
            down = lax.slice_in_dim(down, half, 2 * half, axis=dim)
        up, down = move(up, axis, 1), move(down, axis, -1)
        wait = yield up, down
        if wait:
            up, down = lax.optimization_barrier((up, down, *wait))[:2]


def in_order(block, arrivals):
    ups, downs = zip(*arrivals)
    return [block, *downs[:-1], ups[-1], downs[-1], *ups[-2::-1]]


def scatter_ring(parts, axis, last=()):
    count = len(parts)
    middle = count // 2
    half = parts[0].shape[-2] // 2

    def low(v):
        return v[..., :half, :]

    def high(v):
        return v[..., half:, :]

    up, down = move(low(parts[middle]), axis, 1), move(high(parts[middle]), axis, -1)
    above, below = parts[middle - 1], parts[middle + 1]
    up = jnp.concatenate([plus(low(above), up), high(above)], axis=-2)
    down = jnp.concatenate([low(below), plus(high(below), down)], axis=-2)
    for d in range(middle - 1, 0, -1):
        if d == 1 and last:
            up, down = after(up, *last), after(down, *last)
        up, down = move(up, axis, 1), move(down, axis, -1)
        if d > 1:
            up, down = plus(up, parts[d - 1]), plus(down, parts[count - d + 1])
    return parts[0].astype(F32) + up.astype(F32) + down.astype(F32)


PIECES = [[(z, x) for z in range(Z)] for x in range(X // 2)]
PIECES += [[(z, X // 2) for z in range(Z // 2)], [(z, X // 2) for z in range(Z // 2, Z)]]
PIECES += [[(z, x) for z in range(Z)] for x in range(X // 2 + 1, X)]


FAR = [(0, 1), (1, 3), (3, 6), (6, 8)]
RESULTS = 4 + len(FAR)


def attention_kernel(mine, slots, key_homes, value_homes, place, q_ref, g_ref, *refs):
    if mine == RING:
        *pieces, pairs, dk, work, sems = refs
        pieces, results = pieces[:-RESULTS], pieces[-RESULTS:]
    else:
        total_ref, table_ref, *results, pairs, dk, work, taps, sems = refs
        results = results[RESULTS:]
    o_ref, dq_ref, dk_ref, dv_ref, *far_refs = results
    pair = pl.program_id(0)

    def gathered(which, p, group):
        lanes = pl.ds(pl.multiple_of(place[2] * LANES, LANES), LANES)
        return pltpu.make_async_copy(
            table_ref.at[:, group, :, lanes],
            pairs.at[p, :, :, pl.ds(which * LANES, LANES)],
            sems.at[p, which],
        )

    def passed(which, p, group):
        jobs = []
        for piece, places in zip(pieces, PIECES):
            for i, (dz, dx) in enumerate(places):
                chip = lax.rem(place[0] + dz, Z) * X + lax.rem(place[1] + dx, X)
                jobs.append(
                    pltpu.make_async_copy(
                        piece.at[i, group],
                        pairs.at[p, pl.ds(chip * CORES, CORES), :, pl.ds(which * LANES, LANES)],
                        sems.at[p, which],
                    )
                )
        return jobs

    def copies(p):
        jobs = [gathered(w, p, i) for i, (w, q) in enumerate(GATHERED) if q == mine[p]]
        for i, (w, q) in enumerate(PASSED):
            if q == mine[p]:
                jobs += passed(w, p, i)
        return jobs

    @pl.when(pair == 0)
    def _():
        for p in range(len(mine)):
            for job in copies(p):
                job.start()

    dk[...] = jnp.zeros_like(dk)
    dv_ref[...] = jnp.zeros_like(dv_ref)

    for p in range(len(mine)):

        @pl.when(pair == p)
        def _(p=p):
            for job in copies(p):
                job.wait()

    left = lax.broadcasted_iota(jnp.int32, (BLOCK, LANES), 1) < HEAD_DIM
    none = jnp.zeros((LANES, LANES), BF16)

    def spread(v):
        zero = jnp.zeros_like(v)
        return jnp.concatenate([jnp.where(left, v, zero), jnp.where(left, zero, v)], axis=0)

    def merge(v):
        return jnp.where(left, v[:BLOCK], v[BLOCK:])

    def dot(a, b, dims):
        return lax.dot_general(a, b, dims, preferred_element_type=F32)

    def add(ref, home, part):
        at = (home // 4, pl.ds(pl.multiple_of(home % 4 * BLOCK, BLOCK), BLOCK), slice(None))
        ref[at] = (ref[at].astype(F32) + part).astype(BF16)

    scale = 1.0 / math.sqrt(HEAD_DIM)

    def visit(b):
        rows = slice(b * BLOCK, (b + 1) * BLOCK)
        both = jnp.concatenate(
            [
                pairs[
                    pair,
                    slots[b, j] // 2,
                    pl.ds(pl.multiple_of(slots[b, j] % 2 * BLOCK, BLOCK), BLOCK),
                    :,
                ]
                for j in range(SEL)
            ],
            axis=0,
        )
        query = spread((q_ref[rows, :].astype(F32) * scale).astype(BF16))
        grad = spread(g_ref[rows, :])
        sides = jnp.concatenate(
            [jnp.concatenate([query, none], axis=1), jnp.concatenate([none, grad], axis=1)], axis=0
        )
        chunks = [slice(c, c + CHUNK) for c in range(0, SEL * BLOCK, CHUNK)]
        keys_here, values_here = slice(0, LANES), slice(LANES, 2 * LANES)
        room = work.at[b % 2]
        top = None
        for c in chunks:
            products = dot(both[c], sides, (((1,), (1,)), ((), ())))
            room[c, :] = products
            highest = jnp.max(products[:, keys_here], axis=0, keepdims=True)
            top = highest if top is None else jnp.maximum(top, highest)
        mass = moment = 0.0
        for c in chunks:
            scores = jnp.exp(room[c, keys_here] - top)
            room[c, keys_here] = scores
            mass = mass + jnp.sum(scores, axis=0, keepdims=True)
            moment = moment + jnp.sum(scores * room[c, values_here], axis=0, keepdims=True)
        inverse = 1.0 / mass
        delta = moment * inverse
        sums = 0.0
        for c in chunks:
            probs = room[c, keys_here] * inverse
            slope = probs * (room[c, values_here] - delta)
            factors = jnp.concatenate([slope.astype(BF16), probs.astype(BF16)], axis=1)
            sums = sums + dot(factors, both[c], (((0,), (0,)), ((), ())))
            parts = dot(factors, sides, (((1,), (0,)), ((), ())))
            for i in range(CHUNK // BLOCK):
                part = slice(i * BLOCK, (i + 1) * BLOCK)
                j = c.start // BLOCK + i
                add(dk, key_homes[b, j], parts[part, :LANES])
                add(dv_ref, value_homes[b, j], parts[part, LANES:])
        dq_ref[rows, :] = (merge(sums[:LANES, :LANES]) * scale).astype(BF16)
        o_ref[rows, :] = merge(sums[LANES:, LANES:]).astype(BF16)

    for b in range(4):
        visit(b)

    for i in range(CHIPS):
        dk_ref[i] = dk[i, :KEPT, :]
        z, x = lax.rem(i % Z + FIRST + place[0], Z), i // Z
        dv_ref[i, ROWS + EXTRA :, :] = dk[z * X + x, KEPT:, :]

    if mine != RING:
        @pl.when(pair == 0)
        def _():
            for c in range(CHANNELS // LANES):
                part = slice(c * LANES, (c + 1) * LANES)
                taps[part] = total_ref[:, part].T
            odd = place[2] == 1
            blank = jnp.zeros((EXTRA, LANES - TAPS), F32)
            fill = jnp.zeros((EXTRA - WIDTH, TAPS), F32)

            def extra(i, carry):
                z, x = lax.rem(i % Z + FIRST + place[0], Z), lax.rem(i // Z + place[1], X)
                chip = z * X + x
                both = taps[pl.ds(pl.multiple_of(chip * 2 * WIDTH, 2 * WIDTH), 2 * WIDTH)]
                mine = jnp.where(odd, both[WIDTH:], both[:WIDTH])
                mine = jnp.concatenate([jnp.concatenate([mine, fill], axis=0), blank], axis=1)
                dv_ref[i, pl.ds(ROWS, EXTRA), :] = mine.astype(BF16)
                return carry

            lax.fori_loop(0, CHIPS, extra, 0)

    for ref, (first, end) in zip(far_refs, FAR):
        for i in range(first, end):
            ref[i - first] = dv_ref[X // 2 * Z + i]


def attention(slots, place, queries, grads, total, table, pieces):
    owner = slots // 2
    z, x = owner // (CORES * X), owner // CORES % X
    dz, dx = (z - place[0]) % Z, (x - place[1]) % X
    inner = owner % CORES * 2 + slots % 2
    key_homes = (z * X + dx) * 4 + inner
    value_homes = (dx * Z + (dz + Z - FIRST) % Z) * 4 + inner
    scalars = (slots, key_homes, value_homes, place)
    any_space = pl.BlockSpec(memory_space=pl.ANY)

    def call(mine, more, specs, held, scratch):
        lane_block = lambda rows: pl.BlockSpec((rows, LANES), lambda p, *_: (0, p + mine[0]))
        chip_block = lambda chips, rows: pl.BlockSpec(
            (chips, rows, LANES), lambda p, *_: (0, 0, p + mine[0])
        )
        shapes = [(ROWS,), (ROWS,), (CHIPS, KEPT), (CHIPS, SENT)]
        shapes += [(end - first, SENT) for first, end in FAR]
        inputs = (*scalars, queries, grads, *more)
        return pl.pallas_call(
            functools.partial(attention_kernel, mine),
            grid_spec=pltpu.PrefetchScalarGridSpec(
                num_scalar_prefetch=len(scalars),
                grid=(len(mine),),
                in_specs=[lane_block(ROWS), lane_block(ROWS), *specs, *[any_space] * len(held)],
                out_specs=[
                    lane_block(*shape) if len(shape) == 1 else chip_block(*shape) for shape in shapes
                ],
                scratch_shapes=[
                    pltpu.VMEM((len(mine), CHIPS * CORES, ROWS // CORES, 2 * LANES), BF16),
                    pltpu.VMEM((CHIPS, ROWS, LANES), BF16),
                    pltpu.VMEM((2, SEL * BLOCK, 2 * LANES), F32),
                    *scratch,
                    pltpu.SemaphoreType.DMA((len(mine), 2)),
                ],
            ),
            out_shape=[jax.ShapeDtypeStruct((*shape, HALF_INNER), BF16) for shape in shapes],
            input_output_aliases={len(inputs) + i: i for i in range(len(held))},
            compiler_params=pltpu.CompilerParams(
                dimension_semantics=("arbitrary",), vmem_limit_bytes=50 * 1024 * 1024
            ),
            cost_estimate=pl.CostEstimate(
                flops=1_600_000_000 * len(mine),
                bytes_accessed=9_000_000 * len(mine),
                transcendentals=530_000 * len(mine),
            ),
            name="attend",
        )(*inputs, *held)

    held = call(RING, pieces, [any_space] * len(pieces), (), ())
    whole = pl.BlockSpec((TAPS, CHANNELS), lambda p, *_: (0, 0))
    return call(
        TABLE, (total, table), [whole, any_space], held, [pltpu.VMEM((CHANNELS, TAPS), F32)]
    )


def conv_kernel(x_ref, g_ref, before_ref, after_ref, w_ref, out_ref, dx_ref, dw_ref, xs, hs):
    frames = x_ref.shape[0]
    xs[0:32] = before_ref[0:32].astype(F32)
    xs[32 : 32 + frames] = x_ref[...].astype(F32)
    xs[32 + frames : 64 + frames] = after_ref[0:32].astype(F32)
    wide = frames + 32
    pre = jnp.zeros((wide, LANES), F32)
    for j in range(KERNEL):
        pre = pre + w_ref[j : j + 1, :] * xs[j + 1 : j + 1 + wide]
    gate = 1.0 / (1.0 + jnp.exp(-pre))
    out_ref[...] = (pre * gate)[16 : 16 + frames].astype(BF16)
    incoming = jnp.concatenate(
        [before_ref[32:48], g_ref[...], after_ref[32:48]], axis=0
    ).astype(F32)
    hidden = (incoming * gate * (1.0 + pre * (1.0 - gate))).astype(BF16).astype(F32)
    hs[...] = hidden
    total = jnp.zeros((frames, LANES), F32)
    for j in range(KERNEL):
        total = total + w_ref[j : j + 1, :] * hs[31 - j : 31 - j + frames]
    dx_ref[...] = total.astype(BF16)
    centre = hidden[16 : 16 + frames]
    for j in range(KERNEL):
        product = xs[j + 17 : j + 17 + frames] * centre
        dw_ref[j : j + 1, :] = jnp.sum(product, axis=0, keepdims=True)
    dw_ref[KERNEL:, :] = jnp.zeros((1, LANES), F32)


def convolve(x, g, before, after, weight):
    frames, channels = x.shape
    block = lambda rows: pl.BlockSpec((rows, LANES), lambda p: (0, p))
    return pl.pallas_call(
        conv_kernel,
        grid=(channels // LANES,),
        in_specs=[block(frames), block(frames), block(48), block(48), block(KERNEL)],
        out_specs=[block(frames), block(frames), block(KERNEL + 1)],
        out_shape=[
            jax.ShapeDtypeStruct((frames, channels), BF16),
            jax.ShapeDtypeStruct((frames, channels), BF16),
            jax.ShapeDtypeStruct((KERNEL + 1, channels), F32),
        ],
        scratch_shapes=[pltpu.VMEM((frames + 64, LANES), F32), pltpu.VMEM((frames + 32, LANES), F32)],
        compiler_params=pltpu.CompilerParams(dimension_semantics=("arbitrary",)),
        cost_estimate=pl.CostEstimate(
            flops=20_000_000, bytes_accessed=1_000_000, transcendentals=120_000
        ),
        name="conv",
    )(x, g, before, after, weight)


def body(queries, keys, values, out_grad, picks, conv_in, conv_weight, conv_grad):
    me = lax.axis_index("ctx")
    core = me % CORES
    my_x = (me // CORES) % X
    my_z = me // (CORES * X)
    frames = queries.shape[1]

    def lanes(which, p, side):
        start = side * HALF_INNER + p * LANES
        return (keys, values)[which][0, :, start : start + LANES]

    table = lax.all_gather(
        jnp.stack([jnp.concatenate([lanes(w, p, 0), lanes(w, p, 1)], axis=1) for w, p in GATHERED]),
        "ctx",
    )
    flip = core == 1
    sides = [jnp.stack([lanes(w, p, side) for w, p in PASSED]) for side in range(CORES)]
    mine = jnp.where(flip, sides[1], sides[0])
    taken = swap_cores(jnp.where(flip, sides[0], sides[1]))
    block = jnp.stack([jnp.where(flip, taken, mine), jnp.where(flip, mine, taken)], axis=1)
    steps = gather_steps(block[None], "z", Z, 2)
    column = [next(steps)]
    for _ in range(Z // 2 - 1):
        column.append(steps.send(None))
    column = in_order(block[None], column)
    middle = Z // 2
    column[middle : middle + 2] = [jnp.concatenate(column[middle : middle + 2], axis=2)]
    column = jnp.concatenate(column)
    steps = gather_steps(column, "x", X, 0)
    pieces = [next(steps)]
    for _ in range(X // 2 - 1):
        pieces.append(steps.send(None))
    pieces = in_order(column, pieces)

    packed = jnp.stack([queries[0], out_grad[0]])
    first, second = packed[:, :, :HALF_INNER], packed[:, :, HALF_INNER:]
    taken = swap_cores(jnp.where(flip, first, second))
    chip = jnp.concatenate([jnp.where(flip, second, first), taken], axis=1)
    slots = jnp.concatenate([picks[0], swap_cores(picks[0])], axis=0)

    ends = CHIPS * CORES - 1
    tail = jnp.concatenate([conv_in[0, frames - 32 :], conv_grad[0, frames - 16 :]], axis=0)
    head = jnp.concatenate([conv_in[0, :32], conv_grad[0, :16]], axis=0)
    before = lax.ppermute(tail, "ctx", [(i, i + 1) for i in range(ends)])
    behind = lax.ppermute(head, "ctx", [(i + 1, i) for i in range(ends)])
    conv_out, conv_dx, partial = convolve(conv_in[0], conv_grad[0], before, behind, conv_weight)

    total = partial + swap_cores(partial)
    total = total + lax.ppermute(total, "dp", [(i, i ^ 1) for i in range(4)])
    total = total + lax.ppermute(total, "dp", [(i, i ^ 2) for i in range(4)])

    attended, query_grad, key_parts, value_parts, *far_parts = attention(
        slots, jnp.stack([my_z, my_x, core]), chip[0], chip[1], total, table, pieces
    )

    key_parts = key_parts.reshape(Z, X, KEPT, HALF_INNER)
    value_parts = value_parts.reshape(X, Z, SENT, HALF_INNER)
    key_sum = lax.psum_scatter(
        key_parts, "ctx", scatter_dimension=0, axis_index_groups=COLUMNS
    )
    key_near = [move(key_sum[1], "x", 1), move(key_sum[2], "x", 2), move(key_sum[3], "x", -1)]
    early = scatter_across([value_parts[d, :FIRST] for d in range(X)], *far_parts[:2]).astype(BF16)
    late = scatter_across([value_parts[d, FIRST:] for d in range(X)], *far_parts[2:]).astype(BF16)
    by_z = [early[d] for d in range(FIRST)] + [late[d] for d in range(Z - FIRST)]
    value_sum = scatter_ring([by_z[(d + Z - FIRST) % Z] for d in range(Z)], "z", (key_sum,))
    key_sum = key_sum[0].astype(F32) + sum(near.astype(F32) for near in key_near)
    key_total = jnp.concatenate([key_sum, value_sum[ROWS + EXTRA :]]).astype(BF16)
    value_total = value_sum[:ROWS].astype(BF16)
    weight_grad = value_sum[ROWS : ROWS + WIDTH, :KERNEL].T / math.sqrt(
        conv_in.shape[0] * lax.axis_size("dp") * frames * CHIPS * CORES
    )

    def whole(own, siblings):
        other = swap_cores(siblings)
        return jnp.concatenate([jnp.where(flip, other, own), jnp.where(flip, own, other)], axis=2)

    early = jnp.stack([attended, query_grad])
    late = jnp.stack([key_total, value_total])
    lower, upper = late[:, :frames], late[:, frames:]
    outputs = whole(
        jnp.concatenate([early[:, :frames], jnp.where(flip, upper, lower)]),
        jnp.concatenate([early[:, frames:], jnp.where(flip, lower, upper)]),
    )
    early, late = outputs[:2], outputs[2:]
    return (
        early[0][None],
        early[1][None],
        late[0][None],
        late[1][None],
        conv_out[None],
        conv_dx[None],
        weight_grad,
    )


def solution(mesh):
    rows = P("dp", "ctx", None)
    return jax.shard_map(
        body,
        mesh=mesh,
        in_specs=(rows, rows, rows, rows, rows, rows, P(), rows),
        out_specs=(rows, rows, rows, rows, rows, rows, P(None, "ctx")),
        check_vma=False,
    )
```

```python
import functools
import math

import jax
import jax.numpy as jnp
from jax import lax
from jax.experimental import pallas as pl
from jax.experimental.pallas import tpu as pltpu
from jax.sharding import PartitionSpec as P

Z, X, CORES = 8, 4, 2
CHIPS = Z * X
BLOCK = 64
HEAD_DIM = 64
LANES = 128
SEL = 16
KERNEL = 31
ROWS = 4 * BLOCK
HALF_INNER = 384
PAIRS = HALF_INNER // LANES
EXTRA = 16
CHUNK = 256
FIRST = 3
GATHERED = [(0, 0), (1, 0), (0, 1), (1, 1)]
PASSED = [(0, 2), (1, 2)]
TABLE, RING = (0, 1), (2,)
TAPS = KERNEL + 1
CHANNELS = 768
WIDTH = CHANNELS // (Z * X * CORES)
TAIL = 32
KEPT = ROWS - TAIL
SENT = ROWS + EXTRA + TAIL
F32, BF16 = jnp.float32, jnp.bfloat16


def index_of(z, x, core):
    return (z * X + x) * CORES + core


PLACES = [(z, x, c) for z in range(Z) for x in range(X) for c in range(CORES)]


def along(axis, shift):
    if axis == "z":
        return [(index_of(z, x, c), index_of((z + shift) % Z, x, c)) for z, x, c in PLACES]
    return [(index_of(z, x, c), index_of(z, (x + shift) % X, c)) for z, x, c in PLACES]


def move(value, axis, shift):
    return lax.ppermute(value, "ctx", along(axis, shift))


COLUMNS = [[index_of(z, x, c) for z in range(Z)] for x in range(X) for c in range(CORES)]


def after(value, *others):
    return lax.optimization_barrier((value, *others))[0]


def swap_cores(value):
    return lax.ppermute(value, "ctx", [(i, i ^ 1) for i in range(CHIPS * CORES)])


def plus(a, b):
    return (a.astype(F32) + b.astype(F32)).astype(BF16)


def scatter_across(parts, far_up, far_down):
    cut = far_up.shape[0]
    above, below = parts[1], parts[3]
    up, down = move(far_up, "x", 1), move(far_down, "x", -1)
    up = jnp.concatenate([plus(above[:cut], up), above[cut:]])
    down = jnp.concatenate([below[:cut], plus(below[cut:], down)])
    up, down = move(up, "x", 1), move(down, "x", -1)
    return parts[0].astype(F32) + up.astype(F32) + down.astype(F32)


def gather_steps(block, axis, count, dim):
    half = block.shape[dim] // 2
    up = down = block
    for step in range(count // 2):
        if step == count // 2 - 1:
            up = lax.slice_in_dim(up, 0, half, axis=dim)
            down = lax.slice_in_dim(down, half, 2 * half, axis=dim)
        up, down = move(up, axis, 1), move(down, axis, -1)
        wait = yield up, down
        if wait:
            up, down = lax.optimization_barrier((up, down, *wait))[:2]


def in_order(block, arrivals):
    ups, downs = zip(*arrivals)
    return [block, *downs[:-1], ups[-1], downs[-1], *ups[-2::-1]]


def scatter_ring(parts, axis, last=()):
    count = len(parts)
    middle = count // 2
    half = parts[0].shape[-2] // 32 * 16

    def low(v):
        return v[..., :half, :]

    def high(v):
        return v[..., half:, :]

    up, down = move(low(parts[middle]), axis, 1), move(high(parts[middle]), axis, -1)
    above, below = parts[middle - 1], parts[middle + 1]
    up = jnp.concatenate([plus(low(above), up), high(above)], axis=-2)
    down = jnp.concatenate([low(below), plus(high(below), down)], axis=-2)
    for d in range(middle - 1, 0, -1):
        if d == 1 and last:
            up, down = after(up, *last), after(down, *last)
        up, down = move(up, axis, 1), move(down, axis, -1)
        if d > 1:
            up, down = plus(up, parts[d - 1]), plus(down, parts[count - d + 1])
    return parts[0].astype(F32) + up.astype(F32) + down.astype(F32)


PIECES = [[(z, x) for z in range(Z)] for x in range(X // 2)]
PIECES += [[(z, X // 2) for z in range(Z // 2)], [(z, X // 2) for z in range(Z // 2, Z)]]
PIECES += [[(z, x) for z in range(Z)] for x in range(X // 2 + 1, X)]


FAR = [(0, 1), (1, 3), (3, 6), (6, 8)]
RESULTS = 4 + len(FAR)


def attention_kernel(mine, slots, key_homes, value_homes, place, q_ref, g_ref, *refs):
    if mine == RING:
        *pieces, pairs, dk, work, sems = refs
        pieces, results = pieces[:-RESULTS], pieces[-RESULTS:]
    else:
        total_ref, table_ref, *results, pairs, dk, work, taps, sems = refs
        results = results[RESULTS:]
    o_ref, dq_ref, dk_ref, dv_ref, *far_refs = results
    pair = pl.program_id(0)

    def gathered(which, p, group):
        lanes = pl.ds(pl.multiple_of(place[2] * LANES, LANES), LANES)
        return pltpu.make_async_copy(
            table_ref.at[:, group, :, lanes],
            pairs.at[p, :, :, pl.ds(which * LANES, LANES)],
            sems.at[p, which],
        )

    def passed(which, p, group):
        jobs = []
        for piece, places in zip(pieces, PIECES):
            for i, (dz, dx) in enumerate(places):
                chip = lax.rem(place[0] + dz, Z) * X + lax.rem(place[1] + dx, X)
                jobs.append(
                    pltpu.make_async_copy(
                        piece.at[i, group],
                        pairs.at[p, pl.ds(chip * CORES, CORES), :, pl.ds(which * LANES, LANES)],
                        sems.at[p, which],
                    )
                )
        return jobs

    def copies(p):
        jobs = [gathered(w, p, i) for i, (w, q) in enumerate(GATHERED) if q == mine[p]]
        for i, (w, q) in enumerate(PASSED):
            if q == mine[p]:
                jobs += passed(w, p, i)
        return jobs

    @pl.when(pair == 0)
    def _():
        for p in range(len(mine)):
            for job in copies(p):
                job.start()

    dk[...] = jnp.zeros_like(dk)
    dv_ref[...] = jnp.zeros_like(dv_ref)

    for p in range(len(mine)):

        @pl.when(pair == p)
        def _(p=p):
            for job in copies(p):
                job.wait()

    left = lax.broadcasted_iota(jnp.int32, (BLOCK, LANES), 1) < HEAD_DIM
    none = jnp.zeros((LANES, LANES), BF16)

    def spread(v):
        zero = jnp.zeros_like(v)
        return jnp.concatenate([jnp.where(left, v, zero), jnp.where(left, zero, v)], axis=0)

    def merge(v):
        return jnp.where(left, v[:BLOCK], v[BLOCK:])

    def dot(a, b, dims):
        return lax.dot_general(a, b, dims, preferred_element_type=F32)

    def add(ref, home, part):
        at = (home // 4, pl.ds(pl.multiple_of(home % 4 * BLOCK, BLOCK), BLOCK), slice(None))
        ref[at] = (ref[at].astype(F32) + part).astype(BF16)

    scale = 1.0 / math.sqrt(HEAD_DIM)

    def visit(b):
        rows = slice(b * BLOCK, (b + 1) * BLOCK)
        both = jnp.concatenate(
            [
                pairs[
                    pair,
                    slots[b, j] // 2,
                    pl.ds(pl.multiple_of(slots[b, j] % 2 * BLOCK, BLOCK), BLOCK),
                    :,
                ]
                for j in range(SEL)
            ],
            axis=0,
        )
        query = spread((q_ref[rows, :].astype(F32) * scale).astype(BF16))
        grad = spread(g_ref[rows, :])
        sides = jnp.concatenate(
            [jnp.concatenate([query, none], axis=1), jnp.concatenate([none, grad], axis=1)], axis=0
        )
        chunks = [slice(c, c + CHUNK) for c in range(0, SEL * BLOCK, CHUNK)]
        keys_here, values_here = slice(0, LANES), slice(LANES, 2 * LANES)
        room = work.at[b % 2]
        top = None
        for c in chunks:
            products = dot(both[c], sides, (((1,), (1,)), ((), ())))
            room[c, :] = products
            highest = jnp.max(products[:, keys_here], axis=0, keepdims=True)
            top = highest if top is None else jnp.maximum(top, highest)
        mass = moment = 0.0
        for c in chunks:
            scores = jnp.exp(room[c, keys_here] - top)
            room[c, keys_here] = scores
            mass = mass + jnp.sum(scores, axis=0, keepdims=True)
            moment = moment + jnp.sum(scores * room[c, values_here], axis=0, keepdims=True)
        inverse = 1.0 / mass
        delta = moment * inverse
        sums = 0.0
        for c in chunks:
            probs = room[c, keys_here] * inverse
            slope = probs * (room[c, values_here] - delta)
            factors = jnp.concatenate([slope.astype(BF16), probs.astype(BF16)], axis=1)
            sums = sums + dot(factors, both[c], (((0,), (0,)), ((), ())))
            parts = dot(factors, sides, (((1,), (0,)), ((), ())))
            for i in range(CHUNK // BLOCK):
                part = slice(i * BLOCK, (i + 1) * BLOCK)
                j = c.start // BLOCK + i
                add(dk, key_homes[b, j], parts[part, :LANES])
                add(dv_ref, value_homes[b, j], parts[part, LANES:])
        dq_ref[rows, :] = (merge(sums[:LANES, :LANES]) * scale).astype(BF16)
        o_ref[rows, :] = merge(sums[LANES:, LANES:]).astype(BF16)

    for b in range(4):
        visit(b)

    for i in range(CHIPS):
        dk_ref[i] = dk[i, :KEPT, :]
        z, x = lax.rem(i % Z + FIRST + place[0], Z), i // Z
        dv_ref[i, ROWS + EXTRA :, :] = dk[z * X + x, KEPT:, :]

    if mine != RING:
        @pl.when(pair == 0)
        def _():
            for c in range(CHANNELS // LANES):
                part = slice(c * LANES, (c + 1) * LANES)
                taps[part] = total_ref[:, part].T
            odd = place[2] == 1
            blank = jnp.zeros((EXTRA, LANES - TAPS), F32)
            fill = jnp.zeros((EXTRA - WIDTH, TAPS), F32)

            def extra(i, carry):
                z, x = lax.rem(i % Z + FIRST + place[0], Z), lax.rem(i // Z + place[1], X)
                chip = z * X + x
                both = taps[pl.ds(pl.multiple_of(chip * 2 * WIDTH, 2 * WIDTH), 2 * WIDTH)]
                mine = jnp.where(odd, both[WIDTH:], both[:WIDTH])
                mine = jnp.concatenate([jnp.concatenate([mine, fill], axis=0), blank], axis=1)
                dv_ref[i, pl.ds(ROWS, EXTRA), :] = mine.astype(BF16)
                return carry

            lax.fori_loop(0, CHIPS, extra, 0)

    for ref, (first, end) in zip(far_refs, FAR):
        for i in range(first, end):
            ref[i - first] = dv_ref[X // 2 * Z + i]


def attention(slots, place, queries, grads, total, table, pieces):
    owner = slots // 2
    z, x = owner // (CORES * X), owner // CORES % X
    dz, dx = (z - place[0]) % Z, (x - place[1]) % X
    inner = owner % CORES * 2 + slots % 2
    key_homes = (z * X + dx) * 4 + inner
    value_homes = (dx * Z + (dz + Z - FIRST) % Z) * 4 + inner
    scalars = (slots, key_homes, value_homes, place)
    any_space = pl.BlockSpec(memory_space=pl.ANY)

    def call(mine, more, specs, held, scratch):
        lane_block = lambda rows: pl.BlockSpec((rows, LANES), lambda p, *_: (0, p + mine[0]))
        chip_block = lambda chips, rows: pl.BlockSpec(
            (chips, rows, LANES), lambda p, *_: (0, 0, p + mine[0])
        )
        shapes = [(ROWS,), (ROWS,), (CHIPS, KEPT), (CHIPS, SENT)]
        shapes += [(end - first, SENT) for first, end in FAR]
        inputs = (*scalars, queries, grads, *more)
        return pl.pallas_call(
            functools.partial(attention_kernel, mine),
            grid_spec=pltpu.PrefetchScalarGridSpec(
                num_scalar_prefetch=len(scalars),
                grid=(len(mine),),
                in_specs=[lane_block(ROWS), lane_block(ROWS), *specs, *[any_space] * len(held)],
                out_specs=[
                    lane_block(*shape) if len(shape) == 1 else chip_block(*shape) for shape in shapes
                ],
                scratch_shapes=[
                    pltpu.VMEM((len(mine), CHIPS * CORES, ROWS // CORES, 2 * LANES), BF16),
                    pltpu.VMEM((CHIPS, ROWS, LANES), BF16),
                    pltpu.VMEM((2, SEL * BLOCK, 2 * LANES), F32),
                    *scratch,
                    pltpu.SemaphoreType.DMA((len(mine), 2)),
                ],
            ),
            out_shape=[jax.ShapeDtypeStruct((*shape, HALF_INNER), BF16) for shape in shapes],
            input_output_aliases={len(inputs) + i: i for i in range(len(held))},
            compiler_params=pltpu.CompilerParams(
                dimension_semantics=("arbitrary",), vmem_limit_bytes=50 * 1024 * 1024
            ),
            cost_estimate=pl.CostEstimate(
                flops=1_600_000_000 * len(mine),
                bytes_accessed=9_000_000 * len(mine),
                transcendentals=530_000 * len(mine),
            ),
            name="attend",
        )(*inputs, *held)

    held = call(RING, pieces, [any_space] * len(pieces), (), ())
    whole = pl.BlockSpec((TAPS, CHANNELS), lambda p, *_: (0, 0))
    return call(
        TABLE, (total, table), [whole, any_space], held, [pltpu.VMEM((CHANNELS, TAPS), F32)]
    )


def conv_kernel(x_ref, g_ref, before_ref, after_ref, w_ref, out_ref, dx_ref, dw_ref, xs, hs):
    frames = x_ref.shape[0]
    xs[0:32] = before_ref[0:32].astype(F32)
    xs[32 : 32 + frames] = x_ref[...].astype(F32)
    xs[32 + frames : 64 + frames] = after_ref[0:32].astype(F32)
    wide = frames + 32
    pre = jnp.zeros((wide, LANES), F32)
    for j in range(KERNEL):
        pre = pre + w_ref[j : j + 1, :] * xs[j + 1 : j + 1 + wide]
    gate = 1.0 / (1.0 + jnp.exp(-pre))
    out_ref[...] = (pre * gate)[16 : 16 + frames].astype(BF16)
    incoming = jnp.concatenate(
        [before_ref[32:48], g_ref[...], after_ref[32:48]], axis=0
    ).astype(F32)
    hidden = (incoming * gate * (1.0 + pre * (1.0 - gate))).astype(BF16).astype(F32)
    hs[...] = hidden
    total = jnp.zeros((frames, LANES), F32)
    for j in range(KERNEL):
        total = total + w_ref[j : j + 1, :] * hs[31 - j : 31 - j + frames]
    dx_ref[...] = total.astype(BF16)
    centre = hidden[16 : 16 + frames]
    for j in range(KERNEL):
        product = xs[j + 17 : j + 17 + frames] * centre
        dw_ref[j : j + 1, :] = jnp.sum(product, axis=0, keepdims=True)
    dw_ref[KERNEL:, :] = jnp.zeros((1, LANES), F32)


def convolve(x, g, before, after, weight):
    frames, channels = x.shape
    block = lambda rows: pl.BlockSpec((rows, LANES), lambda p: (0, p))
    return pl.pallas_call(
        conv_kernel,
        grid=(channels // LANES,),
        in_specs=[block(frames), block(frames), block(48), block(48), block(KERNEL)],
        out_specs=[block(frames), block(frames), block(KERNEL + 1)],
        out_shape=[
            jax.ShapeDtypeStruct((frames, channels), BF16),
            jax.ShapeDtypeStruct((frames, channels), BF16),
            jax.ShapeDtypeStruct((KERNEL + 1, channels), F32),
        ],
        scratch_shapes=[pltpu.VMEM((frames + 64, LANES), F32), pltpu.VMEM((frames + 32, LANES), F32)],
        compiler_params=pltpu.CompilerParams(dimension_semantics=("arbitrary",)),
        cost_estimate=pl.CostEstimate(
            flops=20_000_000, bytes_accessed=1_000_000, transcendentals=120_000
        ),
        name="conv",
    )(x, g, before, after, weight)


def body(queries, keys, values, out_grad, picks, conv_in, conv_weight, conv_grad):
    me = lax.axis_index("ctx")
    core = me % CORES
    my_x = (me // CORES) % X
    my_z = me // (CORES * X)
    frames = queries.shape[1]

    def lanes(which, p, side):
        start = side * HALF_INNER + p * LANES
        return (keys, values)[which][0, :, start : start + LANES]

    table = lax.all_gather(
        jnp.stack([jnp.concatenate([lanes(w, p, 0), lanes(w, p, 1)], axis=1) for w, p in GATHERED]),
        "ctx",
    )
    flip = core == 1
    sides = [jnp.stack([lanes(w, p, side) for w, p in PASSED]) for side in range(CORES)]
    mine = jnp.where(flip, sides[1], sides[0])
    taken = swap_cores(jnp.where(flip, sides[0], sides[1]))
    block = jnp.stack([jnp.where(flip, taken, mine), jnp.where(flip, mine, taken)], axis=1)
    steps = gather_steps(block[None], "z", Z, 2)
    column = [next(steps)]
    for _ in range(Z // 2 - 1):
        column.append(steps.send(None))
    column = in_order(block[None], column)
    middle = Z // 2
    column[middle : middle + 2] = [jnp.concatenate(column[middle : middle + 2], axis=2)]
    column = jnp.concatenate(column)
    steps = gather_steps(column, "x", X, 0)
    pieces = [next(steps)]
    for _ in range(X // 2 - 1):
        pieces.append(steps.send(None))
    pieces = in_order(column, pieces)

    packed = jnp.stack([queries[0], out_grad[0]])
    first, second = packed[:, :, :HALF_INNER], packed[:, :, HALF_INNER:]
    taken = swap_cores(jnp.where(flip, first, second))
    chip = jnp.concatenate([jnp.where(flip, second, first), taken], axis=1)
    slots = jnp.concatenate([picks[0], swap_cores(picks[0])], axis=0)

    ends = CHIPS * CORES - 1
    tail = jnp.concatenate([conv_in[0, frames - 32 :], conv_grad[0, frames - 16 :]], axis=0)
    head = jnp.concatenate([conv_in[0, :32], conv_grad[0, :16]], axis=0)
    before = lax.ppermute(tail, "ctx", [(i, i + 1) for i in range(ends)])
    behind = lax.ppermute(head, "ctx", [(i + 1, i) for i in range(ends)])
    conv_out, conv_dx, partial = convolve(conv_in[0], conv_grad[0], before, behind, conv_weight)

    total = partial + swap_cores(partial)
    total = total + lax.ppermute(total, "dp", [(i, i ^ 1) for i in range(4)])
    total = total + lax.ppermute(total, "dp", [(i, i ^ 2) for i in range(4)])

    attended, query_grad, key_parts, value_parts, *far_parts = attention(
        slots, jnp.stack([my_z, my_x, core]), chip[0], chip[1], total, table, pieces
    )

    key_parts = key_parts.reshape(Z, X, KEPT, HALF_INNER)
    value_parts = value_parts.reshape(X, Z, SENT, HALF_INNER)
    key_sum = lax.psum_scatter(
        key_parts, "ctx", scatter_dimension=0, axis_index_groups=COLUMNS
    )
    key_near = [move(key_sum[1], "x", 1), move(key_sum[2], "x", 2), move(key_sum[3], "x", -1)]
    early = scatter_across([value_parts[d, :FIRST] for d in range(X)], *far_parts[:2]).astype(BF16)
    late = scatter_across([value_parts[d, FIRST:] for d in range(X)], *far_parts[2:]).astype(BF16)
    by_z = [early[d] for d in range(FIRST)] + [late[d] for d in range(Z - FIRST)]
    value_sum = scatter_ring([by_z[(d + Z - FIRST) % Z] for d in range(Z)], "z", (key_sum,))
    key_sum = key_sum[0].astype(F32) + sum(near.astype(F32) for near in key_near)
    key_total = jnp.concatenate([key_sum, value_sum[ROWS + EXTRA :]]).astype(BF16)
    value_total = value_sum[:ROWS].astype(BF16)
    weight_grad = value_sum[ROWS : ROWS + WIDTH, :KERNEL].T / math.sqrt(
        conv_in.shape[0] * lax.axis_size("dp") * frames * CHIPS * CORES
    )

    def whole(own, siblings):
        other = swap_cores(siblings)
        return jnp.concatenate([jnp.where(flip, other, own), jnp.where(flip, own, other)], axis=2)

    early = jnp.stack([attended, query_grad])
    early = whole(early[:, :frames], early[:, frames:])
    late = jnp.stack([key_total, value_total])
    lower, upper = late[:, :frames], late[:, frames:]
    late = whole(jnp.where(flip, upper, lower), jnp.where(flip, lower, upper))
    return (
        early[0][None],
        early[1][None],
        late[0][None],
        late[1][None],
        conv_out[None],
        conv_dx[None],
        weight_grad,
    )


def solution(mesh):
    rows = P("dp", "ctx", None)
    return jax.shard_map(
        body,
        mesh=mesh,
        in_specs=(rows, rows, rows, rows, rows, rows, P(), rows),
        out_specs=(rows, rows, rows, rows, rows, rows, P(None, "ctx")),
        check_vma=False,
    )
```
